128 devices in a mesh: leaf: 32 (over y, z, core), sub: 4 (over x).
Axes of the slice: x: 4, y: 4, z: 4, core: 2. Of those that a mesh axis runs over, the one named last changes fastest.
Arguments:
- probe: bfloat16 [8192, 16, 256], P(('leaf', 'sub')), may hold values from -6 to 6
- weights: bfloat16 [8192, 16, 256], P(('leaf', 'sub')), may hold values from -6 to 6
- points: bfloat16 [8192, 3, 256], P(('leaf', 'sub')), may hold values from -3 to 3
- skeleton: bfloat16 [8192, 192], P(('leaf', 'sub')), may hold values from -3 to 3
- row_basis: bfloat16 [8192, 64, 256], P(('leaf', 'sub')), may hold values from -0.75 to 0.75
- col_basis: bfloat16 [8192, 64, 256], P(('leaf', 'sub')), may hold values from -0.375 to 0.375
- near_leaf: int32 [8192, 12], P(('leaf', 'sub')), may hold values from 0 to 8191, as said below
- far_slot: int32 [8192, 64], P(('leaf', 'sub')), may hold values from 0 to 511, as said below
- send_leaf: int32 [128, 128, 4], P(('leaf', 'sub')), may hold values from 0 to 63, as said below
Outputs:
- product: float32 [8192, 16, 256], P(('leaf', 'sub'))
- adjoint: float32 [8192, 16, 256], P(('leaf', 'sub'))
The draws below stay inside these ranges and needn't reach their ends.
Inputs may be any that keep to these rules, and one draw needn't show every extreme that they name: `near_leaf`: entry 0 of a leaf's list is the leaf itself; every entry lies within 8 leaves of it in the global order. `far_slot`: A slot s stands for slot s % 4 of what device s // 4 of leaf+sub sends to the leaf's device. `send_leaf`: leaves are counted within the sending device; for one sender and one receiver the 4 entries differ.
All inputs are finite; a program needn't handle non-finite values.
Results may differ from the reference program's by a relative error of at most 0.0085.
Values may be sent and summed in bfloat16 or wider, within the bound.
A program may use at most 256 MiB of HBM per device.

```python
import jax
import jax.numpy as jnp
from jax import lax

LEAF = 256
RANK = 64
NRHS = 16
LEAF_DEV = 64
NNEAR = 12
NEAR_REACH = 8
NFAR = 64
CAP = 4
LEAVES = 8192
DEVICES = 128


def far_plan(key):
    keys = jax.random.split(key, 5)
    half_cap = max(CAP // 2, 1)
    hot_recv = jax.random.randint(keys[0], (DEVICES,), 0, 2)
    hot_count = jax.random.randint(keys[1], (DEVICES, DEVICES), half_cap, CAP + 1)
    cold_count = jax.random.randint(keys[2], (DEVICES, DEVICES), 1, half_cap + 1)
    live_count = jnp.where(hot_recv[:, None] == 1, hot_count, cold_count)
    device_ids = jnp.arange(DEVICES, dtype=jnp.int32)
    full_pair = (device_ids[None, :] == device_ids[:, None]) | (device_ids[None, :] == DEVICES - 1)
    live_count = jnp.where(full_pair, CAP, live_count)
    leaf_ids = jnp.arange(LEAF_DEV, dtype=jnp.int32)
    scores = jax.random.randint(keys[3], (DEVICES, DEVICES, LEAF_DEV), 0, 1 << 16) * LEAF_DEV + leaf_ids
    chosen = jnp.argsort(scores, axis=-1, stable=True)[..., :CAP].astype(jnp.int32)
    slot_ids = jnp.arange(CAP, dtype=jnp.int32)
    live = (slot_ids[None, None, :] < live_count[:, :, None]).reshape(DEVICES, DEVICES * CAP)
    flat_ids = jnp.arange(DEVICES * CAP, dtype=jnp.int32)
    mixed = jax.random.randint(keys[4], (DEVICES, DEVICES * CAP), 0, 1 << 12) * (DEVICES * CAP) + flat_ids
    keyed = jnp.where(live, mixed, mixed + (1 << 12) * (DEVICES * CAP))
    live_first = jnp.argsort(keyed, axis=-1, stable=True).astype(jnp.int32)
    live_total = jnp.sum(live.astype(jnp.int32), axis=-1)
    position = leaf_ids[:, None] * NFAR + jnp.arange(NFAR, dtype=jnp.int32)[None, :]
    picked = position[None, :, :] % live_total[:, None, None]
    far_lists = jax.vmap(lambda order_row, pick_rows: order_row[pick_rows])(live_first, picked)
    return (chosen, far_lists.reshape(LEAVES, NFAR).astype(jnp.int32))


def draw_send_leaf(key, part):
    plan_pair = far_plan(key)
    return plan_pair[0]


def draw_far_slot(key, part):
    plan_pair = far_plan(key)
    return plan_pair[1]


def draw_near_leaf(key, part):
    key = jax.random.fold_in(key, 11)
    span_all = 2 * NEAR_REACH
    candidate = jnp.arange(span_all, dtype=jnp.int32)
    offsets_all = jnp.where(candidate < NEAR_REACH, candidate - NEAR_REACH, candidate - NEAR_REACH + 1)
    scores = jax.random.randint(key, (LEAVES, span_all), 0, 1 << 16) * span_all + candidate
    chosen = jnp.argsort(scores, axis=1, stable=True)[:, :NNEAR - 1]
    offsets = offsets_all[chosen]
    own_ids = jnp.arange(LEAVES, dtype=jnp.int32)[:, None]
    target = own_ids + offsets
    target = jnp.where((target < 0) | (target >= LEAVES), own_ids - offsets, target)
    return jnp.concatenate([own_ids, target], axis=1).astype(jnp.int32)


def block_levels(key, dims, cuts, low, top_value):
    gain = 1.0
    for axis_at, shards_of in cuts:
        draws = jax.random.uniform(jax.random.fold_in(jax.random.fold_in(key, 6), axis_at), (shards_of,), jnp.float32, low / len(cuts), top_value / len(cuts))
        gain = gain * jnp.repeat(jnp.exp(draws), dims[axis_at] // shards_of).reshape((-1,) + (1,) * (len(dims) - 1 - axis_at))
    return gain


def gaussian(key, shape, spread, most, cuts=(), held_as=jnp.bfloat16):
    result = jax.random.normal(key, shape, jnp.float32) * spread
    if len(cuts) > 0:
        result = block_levels(key, shape, cuts, -0.22, 0.18) * result
    return jnp.clip(result, min=-most, max=most).astype(held_as)


def setup_inputs(seed: int = 0) -> dict:
    key_list = jax.random.split(jax.random.key(seed), 10)
    return {
        "probe": gaussian(key_list[0], (LEAVES, NRHS, LEAF), 1.0, 6.0, ((0, 128),)),
        "weights": gaussian(key_list[1], (LEAVES, NRHS, LEAF), 1.0, 6.0, ((0, 128),)),
        "points": gaussian(key_list[2], (LEAVES, 3, LEAF), 0.5, 3.0, ((0, 128),)),
        "skeleton": gaussian(key_list[3], (LEAVES, 3 * RANK), 0.5, 3.0, ((0, 128),)),
        "row_basis": gaussian(key_list[4], (LEAVES, RANK, LEAF), RANK ** -0.5, 0.75, ((0, 128),)),
        "col_basis": gaussian(key_list[5], (LEAVES, RANK, LEAF), LEAF ** -0.5, 0.375, ((0, 128),)),
        "near_leaf": draw_near_leaf(jax.random.fold_in(key_list[9], 71), 0),
        "far_slot": draw_far_slot(jax.random.fold_in(key_list[9], 71), 0),
        "send_leaf": draw_send_leaf(jax.random.fold_in(key_list[9], 71), 0),
    }


AMPLITUDE = 0.5
LENGTH_SCALE = 0.5
SOFTENING = 0.01
NUGGET = 0.5

def matern(distance_sq):
    scaled = jnp.sqrt(distance_sq + SOFTENING) * (3.0 ** 0.5 / LENGTH_SCALE)
    return AMPLITUDE * (1.0 + scaled) * jnp.exp(-scaled)

def sq_dist(left_xyz, right_xyz):
    total = jnp.zeros(left_xyz.shape[:-2] + (left_xyz.shape[-1], right_xyz.shape[-1]), left_xyz.dtype)
    for comp in range(3):
        offset_comp = left_xyz[..., comp, :, None] - right_xyz[..., comp, None, :]
        total = total + offset_comp * offset_comp
    return total

def round_keep(values):
    return lax.optimization_barrier(values.astype(jnp.bfloat16)).astype(jnp.float32)

def reference(probe, weights, points, skeleton, row_basis, col_basis, near_leaf, far_slot, send_leaf):
    leaves = probe.shape[0]
    coef = jnp.einsum('lka,lra->lkr', col_basis.astype(jnp.float32), probe.astype(jnp.float32))
    coef = round_keep(coef)
    back_coef = jnp.einsum('lka,lra->lkr', row_basis.astype(jnp.float32), weights.astype(jnp.float32))
    back_coef = round_keep(back_coef)
    owner_dev = (jnp.arange(leaves, dtype=jnp.int32) // LEAF_DEV)[:, None]
    sender = far_slot // CAP
    slot_pos = far_slot % CAP
    far_leaf = (sender * LEAF_DEV + send_leaf[sender, owner_dev, slot_pos]).astype(jnp.int32)
    point_xyz = points.astype(jnp.float32)
    skel_xyz = skeleton.astype(jnp.float32).reshape(leaves, 3, RANK)
    probe_f = probe.astype(jnp.float32)
    weights_f = weights.astype(jnp.float32)
    row_f = row_basis.astype(jnp.float32)
    identity_mat = jnp.eye(LEAF, dtype=jnp.float32)
    block_rows = 16

    def group_step(state_pair, begin_row):
        adjoint_near, far_sum = state_pair
        row_ids = begin_row + jnp.arange(block_rows, dtype=jnp.int32)
        near_ids = lax.dynamic_slice_in_dim(near_leaf, begin_row, block_rows, 0)
        own_xyz = lax.dynamic_slice_in_dim(point_xyz, begin_row, block_rows, 0)
        near_kernel = matern(sq_dist(own_xyz[:, None], point_xyz[near_ids]))
        self_mask = (near_ids == row_ids[:, None]).astype(jnp.float32)
        near_kernel = round_keep(near_kernel + NUGGET * self_mask[:, :, None, None] * identity_mat)
        forward = jnp.einsum('gmab,gmrb->gra', near_kernel, probe_f[near_ids])
        own_w = lax.dynamic_slice_in_dim(weights_f, begin_row, block_rows, 0)
        pushed = jnp.einsum('gmab,gra->gmrb', near_kernel, own_w)
        adjoint_near = adjoint_near.at[near_ids.reshape(-1)].add(pushed.reshape(-1, NRHS, LEAF))
        far_ids = lax.dynamic_slice_in_dim(far_leaf, begin_row, block_rows, 0)
        own_skel = lax.dynamic_slice_in_dim(skel_xyz, begin_row, block_rows, 0)
        coupling = round_keep(matern(sq_dist(own_skel[:, None], skel_xyz[far_ids])))
        gathered = round_keep(jnp.einsum('gmkl,gmlr->gkr', coupling, coef[far_ids]))
        own_back = lax.dynamic_slice_in_dim(back_coef, begin_row, block_rows, 0)
        returned = jnp.einsum('gmkl,gkr->gmlr', coupling, own_back)
        far_sum = far_sum.at[far_ids.reshape(-1)].add(returned.reshape(-1, RANK, NRHS))
        own_row = lax.dynamic_slice_in_dim(row_f, begin_row, block_rows, 0)
        product_rows = forward + jnp.einsum('gkr,gka->gra', gathered, own_row)
        return ((adjoint_near, far_sum), product_rows)
    begins = jnp.arange(0, leaves, block_rows, dtype=jnp.int32)
    initial = (jnp.zeros((leaves, NRHS, LEAF), jnp.float32), jnp.zeros((leaves, RANK, NRHS), jnp.float32))
    (adjoint_near, far_sum), product_rows = lax.scan(group_step, initial, begins)
    product = product_rows.reshape(leaves, NRHS, LEAF)
    far_returned = round_keep(far_sum)
    adjoint = adjoint_near + jnp.einsum('lkr,lka->lra', far_returned, col_basis.astype(jnp.float32))
    return (product, adjoint)
```

```python
import functools

import jax
import jax.numpy as jnp
from jax import lax
from jax.experimental import pallas as pl
from jax.experimental.pallas import tpu as pltpu
from jax.sharding import PartitionSpec as P

REACH = 8
SCALE = 3.0**0.5 / 0.5
LOG2E = 1.4426950408889634
SOFTENING = 0.01
NUGGET = 0.5
LEAVES = 64
EXT = LEAVES + 2 * REACH
BAND = REACH + 1
RHS = 16
SIZE = 256
RANK = 64
CAP = 4
PEERS = 128
SLOTS = PEERS * CAP
FAR = 64
bf16 = jnp.bfloat16
f32 = jnp.float32
VMEM = pl.BlockSpec(memory_space=pltpu.VMEM)
SMEM = pl.BlockSpec(memory_space=pltpu.SMEM)


def params(mib=60):
    return pltpu.CompilerParams(vmem_limit_bytes=mib * 2**20)


def kappa(v):
    s = v * lax.rsqrt(v)
    return ((s * (0.5 * SCALE) + 0.5) * jnp.exp2(s * (-SCALE * LOG2E))).astype(bf16)


def split3(n):
    a = n.astype(bf16).astype(f32)
    b = (n - a).astype(bf16).astype(f32)
    return a, b, n - a - b


def stack_rows(rows, height, width):
    at = lax.broadcasted_iota(jnp.int32, (height, width), 0)
    out = jnp.zeros((height, width), f32)
    for r, value in enumerate(rows):
        out = jnp.where(at == r, value, out)
    return out


def point_features(xyz):
    x, y, z = xyz
    n = x * x + y * y + z * z
    one = jnp.ones_like(x)
    right = [x, y, z, *split3(n), one, one, one]
    left = [-2.0 * x, -2.0 * y, -2.0 * z, one, one, one, *split3(n + SOFTENING)]
    return left, right


def prep_kernel(probe, weights, sk, row_basis, col_basis, send, out, back, own, coef_t, feat_t):
    low = lax.broadcasted_iota(jnp.int32, (RHS, 128), 1) < RANK
    low8 = lax.broadcasted_iota(jnp.int32, (8, 128), 1) < RANK

    def leaf(j, _):
        nt = (((1,), (1,)), ((), ()))
        c = lax.dot_general(probe[j], col_basis[j], nt, preferred_element_type=f32)
        coef_t[j] = jnp.concatenate([c, c], axis=1).astype(bf16)
        b = lax.dot_general(weights[j], row_basis[j], nt, preferred_element_type=f32)
        back[j] = b.astype(bf16)
        rows = sk[j].astype(f32)
        left, right = point_features((rows[0:1], rows[1:2], rows[2:3]))
        feat_t[j] = stack_rows(right[:8], 8, 128)
        own[j] = stack_rows(left, 128, 128)[:, :RANK].T.astype(bf16)
        return 0

    lax.fori_loop(0, LEAVES, leaf, 0)

    def peer(d, _):
        at = [send[d * CAP + q] for q in range(CAP)]
        for h in range(2):
            out[d, :, h * 128 : (h + 1) * 128] = jnp.where(low, coef_t[at[2 * h]], coef_t[at[2 * h + 1]])
        f = [jnp.where(low8, feat_t[at[2 * h]], feat_t[at[2 * h + 1]]) for h in range(2)]
        out[d, :, 256:384] = jnp.concatenate(f, axis=0).astype(bf16)
        return 0

    lax.fori_loop(0, PEERS, peer, 0)


def prep(probe, weights, sk, row_basis, col_basis, send):
    return pl.pallas_call(
        prep_kernel,
        out_shape=(
            jax.ShapeDtypeStruct((PEERS, RHS, 384), bf16),
            jax.ShapeDtypeStruct((LEAVES, RHS, RANK), bf16),
            jax.ShapeDtypeStruct((LEAVES, RANK, 128), bf16),
        ),
        in_specs=[VMEM] * 5 + [SMEM],
        out_specs=(VMEM,) * 3,
        scratch_shapes=[pltpu.VMEM((LEAVES, RHS, 128), bf16), pltpu.VMEM((LEAVES, 8, 128), f32)],
        compiler_params=params(),
        name="prep",
    )(probe, weights, sk, row_basis, col_basis, send)


def near_kernel(ext, cf, cb, out, ks, va, acc, left_t, right_t):
    acc[...] = jnp.zeros_like(acc)

    def features(j):
        rows = ext[j, 32:48, :].astype(f32)
        left, right = point_features((rows[0:1], rows[1:2], rows[2:3]))
        right_t[j] = stack_rows(right, 16, SIZE).astype(bf16)
        left_t[j] = stack_rows(left, 128, SIZE).T.astype(bf16)

    def first(j, _):
        features(j)
        return 0

    lax.fori_loop(0, BAND, first, 0)

    def body(j, _):
        right = right_t[j]
        vj = ext[j, 0:32, :]
        for b in range(BAND):
            i = j - REACH + b
            v = jnp.dot(left_t[i, :, 0:16], right, preferred_element_type=f32)
            ks[b * SIZE : (b + 1) * SIZE, :] = kappa(v)
        for b in range(BAND):
            i = j - REACH + b
            d = REACH - b
            c1 = cf[i * BAND + d].astype(bf16)
            c2 = cb[i * BAND + d].astype(bf16)
            vi = ext[i, 0:32, :]
            va[0:16, b * SIZE : (b + 1) * SIZE] = vi[0:16] * c2
            va[16:32, b * SIZE : (b + 1) * SIZE] = vi[16:32] * c1
            if b < REACH:
                vb = jnp.concatenate([vj[0:16] * c1, vj[16:32] * c2], axis=0)
                acc[i] += lax.dot_general(
                    vb, ks[b * SIZE : (b + 1) * SIZE, :], (((1,), (1,)), ((), ())), preferred_element_type=f32
                )
        acc[j] += jnp.dot(va[...], ks[...], preferred_element_type=f32) + (NUGGET * cf[j * BAND]) * vj.astype(f32)
        features(jnp.minimum(j + 1, EXT - 1))
        return 0

    lax.fori_loop(REACH, EXT, body, 0)
    out[...] = acc[REACH : REACH + LEAVES]


def near(ext, cf, cb):
    return pl.pallas_call(
        near_kernel,
        out_shape=jax.ShapeDtypeStruct((LEAVES, 2 * RHS, SIZE), f32),
        in_specs=[VMEM, SMEM, SMEM],
        out_specs=VMEM,
        scratch_shapes=[
            pltpu.VMEM((BAND * SIZE, SIZE), bf16),
            pltpu.VMEM((2 * RHS, BAND * SIZE), bf16),
            pltpu.VMEM((EXT, 2 * RHS, SIZE), f32),
            pltpu.VMEM((EXT, SIZE, 128), bf16),
            pltpu.VMEM((EXT, 16, SIZE), bf16),
        ],
        compiler_params=params(),
        name="near",
    )(ext, cf, cb)


def far_kernel(arrived, own, back, slot, far_in, ret, feat, coef, gt, ct, ks, rt, acc_l, acc_u):
    low = lax.broadcasted_iota(jnp.int32, (RHS, 128), 1) < RANK
    low8 = lax.broadcasted_iota(jnp.int32, (8, 128), 1) < RANK
    tail = jnp.where(lax.broadcasted_iota(jnp.int32, (8, 128), 0) == 0, 1.0, 0.0).astype(f32)

    def both(x, mask):
        y = pltpu.roll(x, RANK, 1)
        return jnp.where(mask, x, y), jnp.where(mask, y, x)

    def table(d, _):
        for h in range(2):
            c = both(arrived[d, :, h * 128 : (h + 1) * 128].astype(f32), low)
            f = both(arrived[d, :, 256:384].astype(f32)[h * 8 : (h + 1) * 8], low8)
            for q in range(2):
                coef[d * CAP + 2 * h + q] = c[q].astype(bf16)
                feat[d * CAP + 2 * h + q] = jnp.concatenate([f[q], tail], axis=0).astype(bf16)
        return 0

    lax.fori_loop(0, PEERS, table, 0)
    acc_l[...] = jnp.zeros_like(acc_l)
    acc_u[...] = jnp.zeros_like(acc_u)

    def leaf(i, _):
        at = [slot[i * FAR + m] for m in range(FAR)]
        for p in range(FAR // 2):
            lanes = slice(p * 128, (p + 1) * 128)
            gt[:, lanes] = jnp.where(low, feat[at[2 * p]], feat[at[2 * p + 1]])
            ct[:, lanes] = jnp.where(low, coef[at[2 * p]], coef[at[2 * p + 1]])
        mine = own[i, :, 0:16]
        for t in range(16):
            lanes = slice(t * 256, (t + 1) * 256)
            ks[:, lanes] = kappa(jnp.dot(mine, gt[:, lanes], preferred_element_type=f32))
        far_in[i] = lax.dot_general(
            ct[...], ks[...], (((1,), (1,)), ((), ())), preferred_element_type=f32
        ).astype(bf16)
        rt[...] = jnp.dot(back[i], ks[...], preferred_element_type=f32)
        for p in range(FAR // 2):
            tile = rt[:, p * 128 : (p + 1) * 128]
            acc_l[at[2 * p]] += tile
            acc_u[at[2 * p + 1]] += tile
        return 0

    lax.fori_loop(0, LEAVES, leaf, 0)

    def pack(d, _):
        for h in range(2):
            s = d * CAP + 2 * h
            even = acc_l[s] + pltpu.roll(acc_u[s], RANK, 1)
            odd = pltpu.roll(acc_l[s + 1], RANK, 1) + acc_u[s + 1]
            ret[d, :, h * 128 : (h + 1) * 128] = jnp.where(low, even, odd).astype(bf16)
        return 0

    lax.fori_loop(0, PEERS, pack, 0)


def far(arrived, own, back, slot):
    return pl.pallas_call(
        far_kernel,
        out_shape=(
            jax.ShapeDtypeStruct((LEAVES, RHS, RANK), bf16),
            jax.ShapeDtypeStruct((PEERS, RHS, 256), bf16),
        ),
        in_specs=[VMEM] * 3 + [SMEM],
        out_specs=(VMEM,) * 2,
        scratch_shapes=[
            pltpu.VMEM((SLOTS, 16, 128), bf16),
            pltpu.VMEM((SLOTS, RHS, 128), bf16),
            pltpu.VMEM((16, FAR * RANK), bf16),
            pltpu.VMEM((RHS, FAR * RANK), bf16),
            pltpu.VMEM((RANK, FAR * RANK), bf16),
            pltpu.VMEM((RHS, FAR * RANK), f32),
            pltpu.VMEM((SLOTS, RHS, 128), f32),
            pltpu.VMEM((SLOTS, RHS, 128), f32),
        ],
        compiler_params=params(),
        name="far",
    )(arrived, own, back, slot)


def post_kernel(came, send, near_out, far_in, row_basis, col_basis, product, adjoint, acc_l, acc_u):
    acc_l[...] = jnp.zeros_like(acc_l)
    acc_u[...] = jnp.zeros_like(acc_u)

    def peer(d, _):
        for h in range(2):
            tile = came[d, :, h * 128 : (h + 1) * 128].astype(f32)
            acc_l[send[d * CAP + 2 * h]] += tile
            acc_u[send[d * CAP + 2 * h + 1]] += tile
        return 0

    lax.fori_loop(0, PEERS, peer, 0)

    def leaf(j, _):
        total = (acc_l[j] + pltpu.roll(acc_u[j], RANK, 1))[:, :RANK].astype(bf16)
        adjoint[j] = near_out[j, RHS:, :] + jnp.dot(total, col_basis[j], preferred_element_type=f32)
        product[j] = near_out[j, :RHS, :] + jnp.dot(far_in[j], row_basis[j], preferred_element_type=f32)
        return 0

    lax.fori_loop(0, LEAVES, leaf, 0)


def post(came, send, near_out, far_in, row_basis, col_basis):
    return pl.pallas_call(
        post_kernel,
        out_shape=(jax.ShapeDtypeStruct((LEAVES, RHS, SIZE), f32),) * 2,
        in_specs=[VMEM, SMEM] + [VMEM] * 4,
        out_specs=(VMEM,) * 2,
        scratch_shapes=[pltpu.VMEM((LEAVES, RHS, 128), f32)] * 2,
        compiler_params=params(),
        name="post",
    )(came, send, near_out, far_in, row_basis, col_basis)


def local(probe, weights, points, skeleton, row_basis, col_basis, near_leaf, far_slot, send_leaf):
    axes = ("leaf", "sub")
    count = lax.axis_size(axes)
    first_leaf = lax.axis_index(axes) * LEAVES
    own_id = first_leaf + jnp.arange(LEAVES, dtype=jnp.int32)
    offsets = jnp.arange(-REACH, REACH + 1, dtype=jnp.int32)
    hits = (near_leaf[:, :, None] - own_id[:, None, None]) == offsets
    counts = jnp.sum(hits.astype(f32), axis=1).astype(bf16)
    counts = jnp.pad(counts, ((0, 0), (0, SIZE - 2 * REACH - 1)))
    block = jnp.concatenate(
        [probe, weights, points, counts[:, None, :], jnp.zeros((LEAVES, 12, SIZE), bf16)], axis=1
    )
    ahead = [(i, i + 1) for i in range(count - 1)]
    behind = [(b, a) for a, b in ahead]
    below = lax.ppermute(block[LEAVES - REACH :], axes, ahead)
    above = lax.ppermute(block[:REACH], axes, behind)
    ext = jnp.concatenate([below, block, above], axis=0)
    cnt = ext[:, 35, : 2 * REACH + 1].astype(f32)
    cf = cnt[: EXT, REACH:]
    cnt_more = jnp.pad(cnt, ((0, REACH), (0, 0)))
    cb = jnp.stack([cnt_more[d : d + EXT, REACH - d] for d in range(BAND)], axis=1)
    send = send_leaf.reshape(SLOTS)
    sk = skeleton.reshape(LEAVES, 3, RANK)
    sk = jnp.concatenate([sk, sk], axis=2)
    payload, back, own = prep(probe, weights, sk, row_basis, col_basis, send)
    arrived = lax.all_to_all(payload, axes, split_axis=0, concat_axis=0, tiled=True)
    near_out = near(ext, cf.reshape(-1), cb.reshape(-1))
    far_in, ret = far(arrived, own, back, far_slot.reshape(-1))
    came = lax.all_to_all(ret, axes, split_axis=0, concat_axis=0, tiled=True)
    return post(came, send, near_out, far_in, row_basis, col_basis)


def solution(mesh):
    lead = P(("leaf", "sub"), None, None)
    flat = P(("leaf", "sub"), None)
    return jax.shard_map(
        local,
        mesh=mesh,
        in_specs=(lead, lead, lead, flat, lead, lead, flat, flat, lead),
        out_specs=(lead, lead),
        check_vma=False,
    )
```

```python
import functools

import jax
import jax.numpy as jnp
from jax import lax
from jax.experimental import pallas as pl
from jax.experimental.pallas import tpu as pltpu
from jax.sharding import PartitionSpec as P

REACH = 8
SCALE = 3.0**0.5 / 0.5
LOG2E = 1.4426950408889634
SOFTENING = 0.01
NUGGET = 0.5
LEAVES = 64
EXT = LEAVES + 2 * REACH
BAND = REACH + 1
RHS = 16
SIZE = 256
RANK = 64
CAP = 4
PEERS = 128
SLOTS = PEERS * CAP
FAR = 64
bf16 = jnp.bfloat16
f32 = jnp.float32
NT = (((1,), (1,)), ((), ()))
MESH = pl.DeviceIdType.MESH
ROWS = 48
FIRST_COLUMNS = 28
VMEM = pl.BlockSpec(memory_space=pltpu.VMEM)
ANY = pl.BlockSpec(memory_space=pl.ANY)
SMEM = pl.BlockSpec(memory_space=pltpu.SMEM)


def params(mib=60, **more):
    return pltpu.CompilerParams(vmem_limit_bytes=mib * 2**20, **more)


def device_id():
    return lax.axis_index("leaf") * 4 + lax.axis_index("sub")


def kappa(v):
    s = v * lax.rsqrt(v)
    return ((s * (0.5 * SCALE) + 0.5) * jnp.exp2(s * (-SCALE * LOG2E))).astype(bf16)


def split3(n):
    a = n.astype(bf16).astype(f32)
    b = (n - a).astype(bf16).astype(f32)
    return a, b, n - a - b


def stack_rows(rows, height, width):
    at = lax.broadcasted_iota(jnp.int32, (height, width), 0)
    out = jnp.zeros((height, width), f32)
    for r, value in enumerate(rows):
        out = jnp.where(at == r, value, out)
    return out


def point_features(xyz):
    x, y, z = xyz
    n = x * x + y * y + z * z
    one = jnp.ones_like(x)
    right = [x, y, z, *split3(n), one, one, one]
    left = [-2.0 * x, -2.0 * y, -2.0 * z, one, one, one, *split3(n + SOFTENING)]
    return left, right


def prep_kernel(
    probe, weights, points, skeleton, row_basis, col_basis, near_leaf, send, out, back, own, block, coef_t, feat_t, sk, cnt
):
    low = lax.broadcasted_iota(jnp.int32, (RHS, 128), 1) < RANK
    low8 = lax.broadcasted_iota(jnp.int32, (8, 128), 1) < RANK
    low64 = lax.broadcasted_iota(jnp.int32, (LEAVES, 128), 1) < RANK
    xy = skeleton[:, 0:128].astype(f32)
    yx = pltpu.roll(xy, RANK, 1)
    sk[0] = jnp.where(low64, xy, yx)
    sk[1] = jnp.where(low64, yx, xy)
    z = skeleton[:, 128:192].astype(f32)
    sk[2] = jnp.concatenate([z, z], axis=1)
    ids = device_id() * LEAVES + lax.broadcasted_iota(jnp.int32, (LEAVES, 128), 0)
    target = ids + lax.broadcasted_iota(jnp.int32, (LEAVES, 128), 1) - REACH
    total = jnp.zeros((LEAVES, 128), f32)
    for m in range(near_leaf.shape[1]):
        total = total + jnp.where(near_leaf[:, m : m + 1] == target, 1.0, 0.0)
    cnt[...] = jnp.where(lax.broadcasted_iota(jnp.int32, (LEAVES, 128), 1) <= 2 * REACH, total, 0.0)

    def leaf(j, _):
        c = lax.dot_general(probe[j], col_basis[j], NT, preferred_element_type=f32)
        coef_t[j] = jnp.concatenate([c, c], axis=1).astype(bf16)
        back[j] = lax.dot_general(weights[j], row_basis[j], NT, preferred_element_type=f32).astype(bf16)
        left, right = point_features(tuple(sk[k, pl.ds(j, 1), :] for k in range(3)))
        feat_t[j] = stack_rows(right[:8], 8, 128)
        own[j] = stack_rows(left, 128, 128)[:, :RANK].T.astype(bf16)
        block[j, 0:16, :] = probe[j]
        block[j, 16:32, :] = weights[j]
        p = points[j].astype(f32)
        n = cnt[pl.ds(j, 1), :]
        rows = [p[0:1], p[1:2], p[2:3], jnp.concatenate([n, jnp.zeros((1, 128), f32)], axis=1)]
        block[j, 32:48, :] = stack_rows(rows, 16, SIZE).astype(bf16)
        return 0

    lax.fori_loop(0, LEAVES, leaf, 0, unroll=4)

    def peer(d, _):
        at = [send[0, d, q] for q in range(CAP)]
        for h in range(2):
            out[d, :, h * 128 : (h + 1) * 128] = jnp.where(low, coef_t[at[2 * h]], coef_t[at[2 * h + 1]])
        f = [jnp.where(low8, feat_t[at[2 * h]], feat_t[at[2 * h + 1]]) for h in range(2)]
        out[d, :, 256:384] = jnp.concatenate(f, axis=0).astype(bf16)
        return 0

    lax.fori_loop(0, PEERS, peer, 0, unroll=4)


def prep(*operands):
    return pl.pallas_call(
        prep_kernel,
        out_shape=(
            jax.ShapeDtypeStruct((PEERS, RHS, 384), bf16),
            jax.ShapeDtypeStruct((LEAVES, RHS, RANK), bf16),
            jax.ShapeDtypeStruct((LEAVES, RANK, 128), bf16),
            jax.ShapeDtypeStruct((LEAVES, ROWS, SIZE), bf16),
        ),
        in_specs=[VMEM] * 7 + [SMEM],
        out_specs=(VMEM,) * 4,
        scratch_shapes=[
            pltpu.VMEM((LEAVES, RHS, 128), bf16),
            pltpu.VMEM((LEAVES, 8, 128), f32),
            pltpu.VMEM((3, LEAVES, 128), f32),
            pltpu.VMEM((LEAVES, 128), f32),
        ],
        compiler_params=params(),
        name="prep",
    )(*operands)


def greet(me):
    barrier = pltpu.get_barrier_semaphore()

    def one(k, _):
        peer = lax.rem(me + k, PEERS)
        pl.semaphore_signal(barrier, inc=1, device_id=(peer // 4, lax.rem(peer, 4)), device_id_type=MESH)
        return 0

    lax.fori_loop(1, PEERS, one, 0)


def all_here():
    pl.semaphore_wait(pltpu.get_barrier_semaphore(), PEERS - 1)


def send_all(me, source, target, send_sem, recv_sem, own_sem):
    pltpu.make_async_copy(source.at[me], target.at[me], own_sem).start()

    def one(k, _):
        peer = lax.rem(me + k, PEERS)
        pltpu.make_async_remote_copy(
            src_ref=source.at[peer],
            dst_ref=target.at[me],
            send_sem=send_sem,
            recv_sem=recv_sem,
            device_id=(peer // 4, lax.rem(peer, 4)),
            device_id_type=MESH,
        ).start()
        return 0

    lax.fori_loop(1, PEERS, one, 0)


def wait_all(me, source, target, send_sem, recv_sem, own_sem):
    pltpu.make_async_copy(source.at[me], target.at[me], own_sem).wait()
    most = pl.ds(0, PEERS - 1)
    pltpu.make_async_copy(source.at[most], source.at[most], send_sem).wait()
    pltpu.make_async_copy(target.at[most], target.at[most], recv_sem).wait()


class Near:
    def __init__(self, vec, cnt, acc, left_t, right_t, ks, kt, va):
        self.vec, self.cnt, self.acc, self.left_t, self.right_t = vec, cnt, acc, left_t, right_t
        self.ks, self.kt, self.va = ks, kt, va

    def features(self, j, tile):
        self.vec[j] = tile[0:32, :]
        rows = tile[32:48, :].astype(f32)
        left, right = point_features((rows[0:1], rows[1:2], rows[2:3]))
        self.right_t[j] = stack_rows(right, 16, SIZE).astype(bf16)
        self.left_t[j] = stack_rows(left, 128, SIZE).T.astype(bf16)
        self.cnt[j] = rows[3:4, 0:128]

    def make(self, j, at):
        right = self.right_t[j]
        for b in range(BAND):
            v = jnp.dot(self.left_t[j - REACH + b, :, 0:16], right, preferred_element_type=f32)
            k = kappa(v)
            self.ks[at][b * SIZE : (b + 1) * SIZE, :] = k
            if b < REACH:
                self.kt[at][b * SIZE : (b + 1) * SIZE, :] = k.T

    def apply(self, j, at):
        ks, kt, va, acc = self.ks[at], self.kt[at], self.va[at], self.acc
        vj = self.vec[j]
        cj = self.cnt[j]

        def spread(c):
            c = jnp.broadcast_to(c, (RHS, 128)).astype(bf16)
            return jnp.concatenate([c, c], axis=1)

        for b in range(BAND):
            i = j - REACH + b
            d = REACH - b
            ahead = spread(self.cnt[i][:, REACH + d : REACH + d + 1])
            behind = spread(cj[:, REACH - d : REACH - d + 1])
            vi = self.vec[i]
            cols = slice(b * SIZE, (b + 1) * SIZE)
            va[0:16, cols] = vi[0:16] * behind
            va[16:32, cols] = vi[16:32] * ahead
            if b < REACH:
                vb = jnp.concatenate([vj[0:16] * ahead, vj[16:32] * behind], axis=0)
                acc[i] += jnp.dot(vb, kt[cols, :], preferred_element_type=f32)
        twice = jnp.broadcast_to(cj[:, REACH : REACH + 1] * NUGGET, (2 * RHS, 128))
        twice = jnp.concatenate([twice, twice], axis=1)
        acc[j] += jnp.dot(va[...], ks[...], preferred_element_type=f32) + twice * vj.astype(f32)


NEAR_SCRATCH = [
    pltpu.VMEM((EXT, 2 * RHS, SIZE), bf16),
    pltpu.VMEM((EXT, 1, 128), f32),
    pltpu.VMEM((EXT, 2 * RHS, SIZE), f32),
    pltpu.VMEM((EXT, SIZE, 128), bf16),
    pltpu.VMEM((EXT, 16, SIZE), bf16),
    pltpu.VMEM((BAND * SIZE, SIZE), bf16),
    pltpu.VMEM((BAND * SIZE, SIZE), bf16),
    pltpu.VMEM((BAND * SIZE, SIZE), bf16),
    pltpu.VMEM((BAND * SIZE, SIZE), bf16),
    pltpu.VMEM((2 * RHS, BAND * SIZE), bf16),
    pltpu.VMEM((2 * RHS, BAND * SIZE), bf16),
]


def near_first_kernel(
    block, payload, block_far, out, arrived, halo, vec, cnt, acc, left_t, right_t, ks0, ks1, kt0, kt1, va0, va1,
    send_sem, recv_sem, own_sem, edge_send, edge_recv
):
    me = device_id()
    greet(me)
    near = Near(vec, cnt, acc, left_t, right_t, (ks0, ks1), (kt0, kt1), (va0, va1))
    acc[...] = jnp.zeros_like(acc)

    def first(j, _):
        near.features(j + REACH, block[j])
        return 0

    lax.fori_loop(0, REACH + FIRST_COLUMNS, first, 0, unroll=4)
    begin = 2 * REACH
    near.make(begin, 0)
    all_here()
    edges = []
    for side in range(2):
        peer = lax.rem(me + (1 if side == 0 else PEERS - 1), PEERS)
        rows = pl.ds(LEAVES - REACH, REACH) if side == 0 else pl.ds(0, REACH)
        edges.append(
            pltpu.make_async_remote_copy(
                src_ref=block_far.at[rows],
                dst_ref=halo.at[pl.ds(side * REACH, REACH)],
                send_sem=edge_send.at[side],
                recv_sem=edge_recv.at[side],
                device_id=(peer // 4, lax.rem(peer, 4)),
                device_id_type=MESH,
            )
        )
        edges[-1].start()
    send_all(me, payload, arrived, send_sem, recv_sem, own_sem)

    def body(g, _):
        j = begin + 2 * g
        near.make(j + 1, 1)
        near.apply(j, 0)
        near.make(j + 2, 0)
        near.apply(j + 1, 1)
        return 0

    lax.fori_loop(0, FIRST_COLUMNS // 2 - 1, body, 0)
    j = begin + FIRST_COLUMNS - 2
    near.make(j + 1, 1)
    near.apply(j, 0)
    near.apply(j + 1, 1)
    out[...] = acc[REACH : REACH + LEAVES]
    for edge in edges:
        edge.wait()
    wait_all(me, payload, arrived, send_sem, recv_sem, own_sem)


def near_first(block, payload):
    return pl.pallas_call(
        near_first_kernel,
        out_shape=(
            jax.ShapeDtypeStruct((LEAVES, 2 * RHS, SIZE), f32),
            jax.ShapeDtypeStruct((PEERS, RHS, 384), bf16),
            jax.ShapeDtypeStruct((2 * REACH, ROWS, SIZE), bf16),
        ),
        in_specs=[VMEM, ANY, ANY],
        out_specs=(VMEM, ANY, ANY),
        scratch_shapes=NEAR_SCRATCH
        + [pltpu.SemaphoreType.DMA] * 3
        + [pltpu.SemaphoreType.DMA((2,)), pltpu.SemaphoreType.DMA((2,))],
        compiler_params=params(collective_id=0, has_side_effects=True),
        name="near_first",
    )(block, payload, block)


def near_rest_kernel(
    block, halo, before, ret, out, came, vec, cnt, acc, left_t, right_t, ks0, ks1, kt0, kt1, va0, va1,
    send_sem, recv_sem, own_sem
):
    me = device_id()
    greet(me)
    near = Near(vec, cnt, acc, left_t, right_t, (ks0, ks1), (kt0, kt1), (va0, va1))

    def edge(j, _):
        near.features(j, halo[j])
        near.features(j + LEAVES + REACH, halo[j + REACH])
        acc[j] = jnp.zeros((2 * RHS, SIZE), f32)
        acc[j + LEAVES + REACH] = jnp.zeros((2 * RHS, SIZE), f32)
        return 0

    lax.fori_loop(0, REACH, edge, 0, unroll=2)

    def first(j, _):
        near.features(j + REACH, block[j])
        acc[j + REACH] = before[j]
        return 0

    lax.fori_loop(0, LEAVES, first, 0, unroll=4)
    begin = 2 * REACH + FIRST_COLUMNS
    upper = EXT - begin
    columns = upper + REACH

    def column(n):
        return jnp.where(n < upper, begin + n, n - upper + REACH)

    near.make(begin, 0)
    all_here()
    send_all(me, ret, came, send_sem, recv_sem, own_sem)

    def body(g, _):
        near.make(column(2 * g + 1), 1)
        near.apply(column(2 * g), 0)
        near.make(column(2 * g + 2), 0)
        near.apply(column(2 * g + 1), 1)
        return 0

    lax.fori_loop(0, columns // 2 - 1, body, 0)
    near.make(column(columns - 1), 1)
    near.apply(column(columns - 2), 0)
    near.apply(column(columns - 1), 1)
    out[...] = acc[REACH : REACH + LEAVES]
    wait_all(me, ret, came, send_sem, recv_sem, own_sem)


def near_rest(block, halo, before, ret):
    return pl.pallas_call(
        near_rest_kernel,
        out_shape=(
            jax.ShapeDtypeStruct((LEAVES, 2 * RHS, SIZE), f32),
            jax.ShapeDtypeStruct((PEERS, RHS, 256), bf16),
        ),
        in_specs=[VMEM, VMEM, VMEM, ANY],
        out_specs=(VMEM, ANY),
        scratch_shapes=NEAR_SCRATCH + [pltpu.SemaphoreType.DMA] * 3,
        compiler_params=params(collective_id=1, has_side_effects=True),
        name="near_rest",
    )(block, halo, before, ret)


def far_kernel(arrived, own, back, slot, far_in, ret, feat, coef, gt, ct0, ct1, ks0, ks1, acc_l, acc_u):
    ct, ks = (ct0, ct1), (ks0, ks1)
    low = lax.broadcasted_iota(jnp.int32, (RHS, 128), 1) < RANK
    low8 = lax.broadcasted_iota(jnp.int32, (8, 128), 1) < RANK
    tail = jnp.where(lax.broadcasted_iota(jnp.int32, (8, 128), 0) == 0, 1.0, 0.0).astype(f32)

    def both(x, mask):
        y = pltpu.roll(x, RANK, 1)
        return jnp.where(mask, x, y), jnp.where(mask, y, x)

    def table(d, _):
        for h in range(2):
            c = both(arrived[d, :, h * 128 : (h + 1) * 128].astype(f32), low)
            f = both(arrived[d, :, 256:384].astype(f32)[h * 8 : (h + 1) * 8], low8)
            for q in range(2):
                coef[d * CAP + 2 * h + q] = c[q].astype(bf16)
                feat[d * CAP + 2 * h + q] = jnp.concatenate([f[q], tail], axis=0).astype(bf16)
        return 0

    lax.fori_loop(0, PEERS, table, 0, unroll=4)
    acc_l[...] = jnp.zeros_like(acc_l)
    acc_u[...] = jnp.zeros_like(acc_u)

    def make(i, p):
        for m in range(FAR // 2):
            lanes = slice(m * 128, (m + 1) * 128)
            a, b = slot[i, 2 * m], slot[i, 2 * m + 1]
            gt[:, lanes] = jnp.where(low, feat[a], feat[b])
            ct[p][:, lanes] = jnp.where(low, coef[a], coef[b])
        mine = own[i, :, 0:16]
        for t in range(16):
            lanes = slice(t * 256, (t + 1) * 256)
            ks[p][:, lanes] = kappa(jnp.dot(mine, gt[:, lanes], preferred_element_type=f32))

    def apply(i, p):
        far_in[i] = lax.dot_general(ct[p][...], ks[p][...], NT, preferred_element_type=f32).astype(bf16)
        rt = jnp.dot(back[i], ks[p][...], preferred_element_type=f32)
        for m in range(FAR // 2):
            tile = rt[:, m * 128 : (m + 1) * 128]
            acc_l[slot[i, 2 * m]] += tile
            acc_u[slot[i, 2 * m + 1]] += tile

    make(0, 0)

    def pair(g, _):
        make(2 * g + 1, 1)
        apply(2 * g, 0)
        make(jnp.minimum(2 * g + 2, LEAVES - 1), 0)
        apply(2 * g + 1, 1)
        return 0

    lax.fori_loop(0, LEAVES // 2, pair, 0)

    def pack(d, _):
        for h in range(2):
            s = d * CAP + 2 * h
            even = acc_l[s] + pltpu.roll(acc_u[s], RANK, 1)
            odd = pltpu.roll(acc_l[s + 1], RANK, 1) + acc_u[s + 1]
            ret[d, :, h * 128 : (h + 1) * 128] = jnp.where(low, even, odd).astype(bf16)
        return 0

    lax.fori_loop(0, PEERS, pack, 0, unroll=4)


def far(arrived, own, back, slot):
    return pl.pallas_call(
        far_kernel,
        out_shape=(
            jax.ShapeDtypeStruct((LEAVES, RHS, RANK), bf16),
            jax.ShapeDtypeStruct((PEERS, RHS, 256), bf16),
        ),
        in_specs=[VMEM] * 3 + [SMEM],
        out_specs=(VMEM,) * 2,
        scratch_shapes=[
            pltpu.VMEM((SLOTS, 16, 128), bf16),
            pltpu.VMEM((SLOTS, RHS, 128), bf16),
            pltpu.VMEM((16, FAR * RANK), bf16),
            pltpu.VMEM((RHS, FAR * RANK), bf16),
            pltpu.VMEM((RHS, FAR * RANK), bf16),
            pltpu.VMEM((RANK, FAR * RANK), bf16),
            pltpu.VMEM((RANK, FAR * RANK), bf16),
            pltpu.VMEM((SLOTS, RHS, 128), f32),
            pltpu.VMEM((SLOTS, RHS, 128), f32),
        ],
        compiler_params=params(),
        name="far",
    )(arrived, own, back, slot)


def post_kernel(came, send, near_out, far_in, row_basis, col_basis, product, adjoint, acc_l, acc_u):
    acc_l[...] = jnp.zeros_like(acc_l)
    acc_u[...] = jnp.zeros_like(acc_u)

    def peer(d, _):
        for h in range(2):
            tile = came[d, :, h * 128 : (h + 1) * 128].astype(f32)
            acc_l[send[0, d, 2 * h]] += tile
            acc_u[send[0, d, 2 * h + 1]] += tile
        return 0

    lax.fori_loop(0, PEERS, peer, 0, unroll=4)

    def leaf(j, _):
        total = (acc_l[j] + pltpu.roll(acc_u[j], RANK, 1))[:, :RANK].astype(bf16)
        adjoint[j] = near_out[j, RHS:, :] + jnp.dot(total, col_basis[j], preferred_element_type=f32)
        product[j] = near_out[j, :RHS, :] + jnp.dot(far_in[j], row_basis[j], preferred_element_type=f32)
        return 0

    lax.fori_loop(0, LEAVES, leaf, 0, unroll=4)


def post(came, send, near_out, far_in, row_basis, col_basis):
    return pl.pallas_call(
        post_kernel,
        out_shape=(jax.ShapeDtypeStruct((LEAVES, RHS, SIZE), f32),) * 2,
        in_specs=[VMEM, SMEM] + [VMEM] * 4,
        out_specs=(VMEM,) * 2,
        scratch_shapes=[pltpu.VMEM((LEAVES, RHS, 128), f32)] * 2,
        compiler_params=params(),
        name="post",
    )(came, send, near_out, far_in, row_basis, col_basis)


def local(probe, weights, points, skeleton, row_basis, col_basis, near_leaf, far_slot, send_leaf):
    payload, back, own, block = prep(
        probe, weights, points, skeleton, row_basis, col_basis, near_leaf, send_leaf
    )
    near_part, arrived, halo = near_first(block, payload)
    far_in, ret = far(arrived, own, back, far_slot)
    near_out, came = near_rest(block, halo, near_part, ret)
    return post(came, send_leaf, near_out, far_in, row_basis, col_basis)


def solution(mesh):
    lead = P(("leaf", "sub"), None, None)
    flat = P(("leaf", "sub"), None)
    return jax.shard_map(
        local,
        mesh=mesh,
        in_specs=(lead, lead, lead, flat, lead, lead, flat, flat, lead),
        out_specs=(lead, lead),
        check_vma=False,
    )
```

```python
import functools

import jax
import jax.numpy as jnp
from jax import lax
from jax.experimental import pallas as pl
from jax.experimental.pallas import tpu as pltpu
from jax.sharding import PartitionSpec as P

REACH = 8
SCALE = 3.0**0.5 / 0.5
LOG2E = 1.4426950408889634
SOFTENING = 0.01
NUGGET = 0.5
LEAVES = 64
EXT = LEAVES + 2 * REACH
BAND = REACH + 1
RHS = 16
SIZE = 256
RANK = 64
CAP = 4
PEERS = 128
SLOTS = PEERS * CAP
FAR = 64
bf16 = jnp.bfloat16
f32 = jnp.float32
NT = (((1,), (1,)), ((), ()))
MESH = pl.DeviceIdType.MESH
ROWS = 48
FIRST_COLUMNS = 28
VMEM = pl.BlockSpec(memory_space=pltpu.VMEM)
ANY = pl.BlockSpec(memory_space=pl.ANY)
SMEM = pl.BlockSpec(memory_space=pltpu.SMEM)


def params(mib=24, **more):
    return pltpu.CompilerParams(vmem_limit_bytes=mib * 2**20, **more)


def device_id():
    return lax.axis_index("leaf") * 4 + lax.axis_index("sub")


def kappa(v):
    s = v * lax.rsqrt(v)
    return ((s * (0.5 * SCALE) + 0.5) * jnp.exp2(s * (-SCALE * LOG2E))).astype(bf16)


def split3(n):
    a = n.astype(bf16).astype(f32)
    b = (n - a).astype(bf16).astype(f32)
    return a, b, n - a - b


def stack_rows(rows, height, width):
    at = lax.broadcasted_iota(jnp.int32, (height, width), 0)
    out = jnp.zeros((height, width), f32)
    for r, value in enumerate(rows):
        out = jnp.where(at == r, value, out)
    return out


def point_features(xyz):
    x, y, z = xyz
    n = x * x + y * y + z * z
    one = jnp.ones_like(x)
    right = [x, y, z, *split3(n), one, one, one]
    left = [-2.0 * x, -2.0 * y, -2.0 * z, one, one, one, *split3(n + SOFTENING)]
    return left, right


def prep_kernel(
    probe, weights, points, skeleton, row_basis, col_basis, near_leaf, send, out, back, own, block, coef_t, feat_t, sk, cnt, pts
):
    low = lax.broadcasted_iota(jnp.int32, (RHS, 128), 1) < RANK
    low8 = lax.broadcasted_iota(jnp.int32, (8, 128), 1) < RANK
    low64 = lax.broadcasted_iota(jnp.int32, (LEAVES, 128), 1) < RANK
    xy = skeleton[:, 0:128].astype(f32)
    yx = pltpu.roll(xy, RANK, 1)
    sk[0] = jnp.where(low64, xy, yx)
    sk[1] = jnp.where(low64, yx, xy)
    z = skeleton[:, 128:192].astype(f32)
    sk[2] = jnp.concatenate([z, z], axis=1)
    ids = device_id() * LEAVES + lax.broadcasted_iota(jnp.int32, (32, LEAVES), 1)
    offset = lax.broadcasted_iota(jnp.int32, (32, LEAVES), 0)
    total = jnp.zeros((32, LEAVES), f32)
    for m in range(near_leaf.shape[0]):
        total = total + jnp.where(near_leaf[m : m + 1, :] == ids + (offset - REACH), 1.0, 0.0)
    total = jnp.where(offset <= 2 * REACH, total, 0.0)
    total = jnp.concatenate([total, total], axis=1)
    cnt[...] = jnp.concatenate([total, jnp.zeros((96, 128), f32)], axis=0).T[0:LEAVES]
    for c in range(3):
        pts[c] = points[c].astype(f32)

    def leaf(j, _):
        c = lax.dot_general(probe[j], col_basis[j], NT, preferred_element_type=f32)
        coef_t[j] = jnp.concatenate([c, c], axis=1).astype(bf16)
        back[j] = lax.dot_general(weights[j], row_basis[j], NT, preferred_element_type=f32).astype(bf16)
        left, right = point_features(tuple(sk[k, pl.ds(j, 1), :] for k in range(3)))
        feat_t[j] = stack_rows(right[:8], 8, 128)
        own[j] = stack_rows(left, 128, 128)[:, :RANK].T.astype(bf16)
        block[j, 0:16, :] = probe[j]
        block[j, 16:32, :] = weights[j]
        n = cnt[pl.ds(j, 1), :]
        rows = [*(pts[c, pl.ds(j, 1), :] for c in range(3)), jnp.concatenate([n, jnp.zeros((1, 128), f32)], axis=1)]
        block[j, 32:48, :] = stack_rows(rows, 16, SIZE).astype(bf16)
        return 0

    lax.fori_loop(0, LEAVES, leaf, 0, unroll=4)

    def peer(d, _):
        at = [send[q, d] for q in range(CAP)]
        for h in range(2):
            out[d, :, h * 128 : (h + 1) * 128] = jnp.where(low, coef_t[at[2 * h]], coef_t[at[2 * h + 1]])
        f = [jnp.where(low8, feat_t[at[2 * h]], feat_t[at[2 * h + 1]]) for h in range(2)]
        out[d, :, 256:384] = jnp.concatenate(f, axis=0).astype(bf16)
        return 0

    lax.fori_loop(0, PEERS, peer, 0, unroll=4)


def prep(*operands):
    return pl.pallas_call(
        prep_kernel,
        out_shape=(
            jax.ShapeDtypeStruct((PEERS, RHS, 384), bf16),
            jax.ShapeDtypeStruct((LEAVES, RHS, RANK), bf16),
            jax.ShapeDtypeStruct((LEAVES, RANK, 128), bf16),
            jax.ShapeDtypeStruct((LEAVES, ROWS, SIZE), bf16),
        ),
        in_specs=[VMEM] * 7 + [SMEM],
        out_specs=(VMEM,) * 4,
        scratch_shapes=[
            pltpu.VMEM((LEAVES, RHS, 128), bf16),
            pltpu.VMEM((LEAVES, 8, 128), f32),
            pltpu.VMEM((3, LEAVES, 128), f32),
            pltpu.VMEM((LEAVES, 128), f32),
            pltpu.VMEM((3, LEAVES, SIZE), f32),
        ],
        compiler_params=params(),
        name="prep",
    )(*operands)


def greet(me):
    barrier = pltpu.get_barrier_semaphore()

    def one(k, _):
        peer = lax.rem(me + k, PEERS)
        pl.semaphore_signal(barrier, inc=1, device_id=(peer // 4, lax.rem(peer, 4)), device_id_type=MESH)
        return 0

    lax.fori_loop(1, PEERS, one, 0)


def all_here():
    pl.semaphore_wait(pltpu.get_barrier_semaphore(), PEERS - 1)


def send_all(me, source, target, send_sem, recv_sem, own_sem):
    pltpu.make_async_copy(source.at[me], target.at[me], own_sem).start()

    def one(k, _):
        peer = lax.rem(me + k, PEERS)
        pltpu.make_async_remote_copy(
            src_ref=source.at[peer],
            dst_ref=target.at[me],
            send_sem=send_sem,
            recv_sem=recv_sem,
            device_id=(peer // 4, lax.rem(peer, 4)),
            device_id_type=MESH,
        ).start()
        return 0

    lax.fori_loop(1, PEERS, one, 0)


def wait_all(me, source, target, send_sem, recv_sem, own_sem):
    pltpu.make_async_copy(source.at[me], target.at[me], own_sem).wait()
    most = pl.ds(0, PEERS - 1)
    pltpu.make_async_copy(source.at[most], source.at[most], send_sem).wait()
    pltpu.make_async_copy(target.at[most], target.at[most], recv_sem).wait()


class Near:
    def __init__(self, vec, cnt, acc, left_t, right_t, ks, kt, va):
        self.vec, self.cnt, self.acc, self.left_t, self.right_t = vec, cnt, acc, left_t, right_t
        self.ks, self.kt, self.va = ks, kt, va

    def features(self, j, tile):
        self.vec[j] = tile[0:32, :]
        rows = tile[32:48, :].astype(f32)
        left, right = point_features((rows[0:1], rows[1:2], rows[2:3]))
        self.right_t[j] = stack_rows(right, 16, SIZE).astype(bf16)
        self.left_t[j] = stack_rows(left, 128, SIZE).T.astype(bf16)
        self.cnt[j] = rows[3:4, 0:128]

    def make(self, j, at, b):
        v = jnp.dot(self.left_t[j - REACH + b, :, 0:16], self.right_t[j], preferred_element_type=f32)
        k = kappa(v)
        self.ks[at][b * SIZE : (b + 1) * SIZE, :] = k
        if b < REACH:
            self.kt[at][b * SIZE : (b + 1) * SIZE, :] = k.T

    def make_all(self, j, at):
        for b in range(BAND):
            self.make(j, at, b)

    def step(self, j, at, j_next=None):
        ks, kt, va, acc = self.ks[at], self.kt[at], self.va[at], self.acc
        vj = self.vec[j]
        cj = self.cnt[j]

        def spread(c, rows=RHS):
            c = jnp.broadcast_to(c, (rows, 128))
            return jnp.concatenate([c, c], axis=1)

        total = spread(cj[:, REACH : REACH + 1] * NUGGET, 2 * RHS) * vj.astype(f32)
        for b in range(BAND):
            i = j - REACH + b
            d = REACH - b
            ahead = spread(self.cnt[i][:, REACH + d : REACH + d + 1]).astype(bf16)
            behind = spread(cj[:, REACH - d : REACH - d + 1]).astype(bf16)
            vi = self.vec[i]
            cols = slice(b * SIZE, (b + 1) * SIZE)
            va[0:16, cols] = vi[0:16] * behind
            va[16:32, cols] = vi[16:32] * ahead
            if b < REACH:
                vb = jnp.concatenate([vj[0:16] * ahead, vj[16:32] * behind], axis=0)
                acc[i] += jnp.dot(vb, kt[cols, :], preferred_element_type=f32)
            if b % 3 == 2:
                cols = slice((b - 2) * SIZE, (b + 1) * SIZE)
                total = total + jnp.dot(va[:, cols], ks[cols, :], preferred_element_type=f32)
            if j_next is not None:
                self.make(j_next, 1 - at, b)
        acc[j] += total


NEAR_SCRATCH = [
    pltpu.VMEM((EXT, 2 * RHS, SIZE), bf16),
    pltpu.VMEM((EXT, 1, 128), f32),
    pltpu.VMEM((EXT, 2 * RHS, SIZE), f32),
    pltpu.VMEM((EXT, SIZE, 128), bf16),
    pltpu.VMEM((EXT, 16, SIZE), bf16),
    pltpu.VMEM((BAND * SIZE, SIZE), bf16),
    pltpu.VMEM((BAND * SIZE, SIZE), bf16),
    pltpu.VMEM((BAND * SIZE, SIZE), bf16),
    pltpu.VMEM((BAND * SIZE, SIZE), bf16),
    pltpu.VMEM((2 * RHS, BAND * SIZE), bf16),
    pltpu.VMEM((2 * RHS, BAND * SIZE), bf16),
]


def near_first_kernel(
    block, payload, block_far, out, arrived, halo, vec, cnt, acc, left_t, right_t, ks0, ks1, kt0, kt1, va0, va1,
    send_sem, recv_sem, own_sem, edge_send, edge_recv
):
    me = device_id()
    greet(me)
    near = Near(vec, cnt, acc, left_t, right_t, (ks0, ks1), (kt0, kt1), (va0, va1))
    acc[...] = jnp.zeros_like(acc)

    def first(j, _):
        near.features(j + REACH, block[j])
        return 0

    lax.fori_loop(0, REACH + FIRST_COLUMNS, first, 0, unroll=4)
    begin = 2 * REACH
    near.make_all(begin, 0)
    all_here()
    edges = []
    for side in range(2):
        peer = lax.rem(me + (1 if side == 0 else PEERS - 1), PEERS)
        rows = pl.ds(LEAVES - REACH, REACH) if side == 0 else pl.ds(0, REACH)
        edges.append(
            pltpu.make_async_remote_copy(
                src_ref=block_far.at[rows],
                dst_ref=halo.at[pl.ds(side * REACH, REACH)],
                send_sem=edge_send.at[side],
                recv_sem=edge_recv.at[side],
                device_id=(peer // 4, lax.rem(peer, 4)),
                device_id_type=MESH,
            )
        )
        edges[-1].start()
    send_all(me, payload, arrived, send_sem, recv_sem, own_sem)

    def body(g, _):
        j = begin + 2 * g
        near.step(j, 0, j + 1)
        near.step(j + 1, 1, j + 2)
        return 0

    lax.fori_loop(0, FIRST_COLUMNS // 2 - 1, body, 0)
    j = begin + FIRST_COLUMNS - 2
    near.step(j, 0, j + 1)
    near.step(j + 1, 1)
    out[...] = acc[REACH : REACH + LEAVES]
    for edge in edges:
        edge.wait()
    wait_all(me, payload, arrived, send_sem, recv_sem, own_sem)


def near_first(block, payload):
    return pl.pallas_call(
        near_first_kernel,
        out_shape=(
            jax.ShapeDtypeStruct((LEAVES, 2 * RHS, SIZE), f32),
            jax.ShapeDtypeStruct((PEERS, RHS, 384), bf16),
            jax.ShapeDtypeStruct((2 * REACH, ROWS, SIZE), bf16),
        ),
        in_specs=[VMEM, ANY, ANY],
        out_specs=(VMEM, ANY, ANY),
        scratch_shapes=NEAR_SCRATCH
        + [pltpu.SemaphoreType.DMA] * 3
        + [pltpu.SemaphoreType.DMA((2,)), pltpu.SemaphoreType.DMA((2,))],
        compiler_params=params(collective_id=0, has_side_effects=True),
        name="near_first",
    )(block, payload, block)


def near_rest_kernel(
    block, halo, before, ret, out, came, vec, cnt, acc, left_t, right_t, ks0, ks1, kt0, kt1, va0, va1,
    send_sem, recv_sem, own_sem
):
    me = device_id()
    greet(me)
    near = Near(vec, cnt, acc, left_t, right_t, (ks0, ks1), (kt0, kt1), (va0, va1))

    def edge(j, _):
        near.features(j, halo[j])
        near.features(j + LEAVES + REACH, halo[j + REACH])
        acc[j] = jnp.zeros((2 * RHS, SIZE), f32)
        acc[j + LEAVES + REACH] = jnp.zeros((2 * RHS, SIZE), f32)
        return 0

    lax.fori_loop(0, REACH, edge, 0, unroll=2)

    def first(j, _):
        near.features(j + REACH, block[j])
        acc[j + REACH] = before[j]
        return 0

    lax.fori_loop(0, LEAVES, first, 0, unroll=4)
    begin = 2 * REACH + FIRST_COLUMNS
    upper = EXT - begin
    columns = upper + REACH

    def column(n):
        return jnp.where(n < upper, begin + n, n - upper + REACH)

    near.make_all(begin, 0)
    all_here()
    send_all(me, ret, came, send_sem, recv_sem, own_sem)

    def body(g, _):
        near.step(column(2 * g), 0, column(2 * g + 1))
        near.step(column(2 * g + 1), 1, column(2 * g + 2))
        return 0

    lax.fori_loop(0, columns // 2 - 1, body, 0)
    near.step(column(columns - 2), 0, column(columns - 1))
    near.step(column(columns - 1), 1)
    out[...] = acc[REACH : REACH + LEAVES]
    wait_all(me, ret, came, send_sem, recv_sem, own_sem)


def near_rest(block, halo, before, ret):
    return pl.pallas_call(
        near_rest_kernel,
        out_shape=(
            jax.ShapeDtypeStruct((LEAVES, 2 * RHS, SIZE), f32),
            jax.ShapeDtypeStruct((PEERS, RHS, 256), bf16),
        ),
        in_specs=[VMEM, VMEM, VMEM, ANY],
        out_specs=(VMEM, ANY),
        scratch_shapes=NEAR_SCRATCH + [pltpu.SemaphoreType.DMA] * 3,
        compiler_params=params(collective_id=1, has_side_effects=True),
        name="near_rest",
    )(block, halo, before, ret)


def far_kernel(arrived, own, back, slot, far_in, ret, feat, coef, gt0, gt1, ct0, ct1, ks0, ks1, acc_l, acc_u):
    gt, ct, ks = (gt0, gt1), (ct0, ct1), (ks0, ks1)
    low = lax.broadcasted_iota(jnp.int32, (RHS, 128), 1) < RANK
    low8 = lax.broadcasted_iota(jnp.int32, (8, 128), 1) < RANK
    tail = jnp.where(lax.broadcasted_iota(jnp.int32, (8, 128), 0) == 0, 1.0, 0.0).astype(f32)

    def both(x, mask):
        y = pltpu.roll(x, RANK, 1)
        return jnp.where(mask, x, y), jnp.where(mask, y, x)

    def table(d, _):
        for h in range(2):
            c = both(arrived[d, :, h * 128 : (h + 1) * 128].astype(f32), low)
            f = both(arrived[d, :, 256:384].astype(f32)[h * 8 : (h + 1) * 8], low8)
            for q in range(2):
                coef[d * CAP + 2 * h + q] = c[q].astype(bf16)
                feat[d * CAP + 2 * h + q] = jnp.concatenate([f[q], tail], axis=0).astype(bf16)
        return 0

    lax.fori_loop(0, PEERS, table, 0, unroll=4)
    acc_l[...] = jnp.zeros_like(acc_l)
    acc_u[...] = jnp.zeros_like(acc_u)

    def gather(i, p, t):
        for m in range(2 * t, 2 * t + 2):
            lanes = slice(m * 128, (m + 1) * 128)
            a, b = slot[i, 2 * m], slot[i, 2 * m + 1]
            gt[p][:, lanes] = jnp.where(low, feat[a], feat[b])
            ct[p][:, lanes] = jnp.where(low, coef[a], coef[b])

    def make(i, p, t):
        lanes = slice(t * 256, (t + 1) * 256)
        ks[p][:, lanes] = kappa(jnp.dot(own[i, :, 0:16], gt[p][:, lanes], preferred_element_type=f32))

    def apply(i, p, t, w):
        lanes = slice(t * 256, (t + w) * 256)
        part = lax.dot_general(ct[p][:, lanes], ks[p][:, lanes], NT, preferred_element_type=f32)
        rt = jnp.dot(back[i], ks[p][:, lanes], preferred_element_type=f32)
        for m in range(2 * w):
            tile = rt[:, m * 128 : (m + 1) * 128]
            acc_l[slot[i, 4 * t + 2 * m]] += tile
            acc_u[slot[i, 4 * t + 2 * m + 1]] += tile
        return part

    TILES = 16
    W = 2

    def step(i_next, p_next, i, p):
        total = None
        for t in range(0, TILES, W):
            part = apply(i, p, t, W)
            total = part if total is None else total + part
            for u in range(t, t + W):
                gather(i_next, p_next, u)
                make(i_next, p_next, u)
        far_in[i] = total.astype(bf16)

    for t in range(TILES):
        gather(0, 0, t)
        make(0, 0, t)

    def pair(g, _):
        step(2 * g + 1, 1, 2 * g, 0)
        step(jnp.minimum(2 * g + 2, LEAVES - 1), 0, 2 * g + 1, 1)
        return 0

    lax.fori_loop(0, LEAVES // 2, pair, 0)

    def pack(d, _):
        for h in range(2):
            s = d * CAP + 2 * h
            even = acc_l[s] + pltpu.roll(acc_u[s], RANK, 1)
            odd = pltpu.roll(acc_l[s + 1], RANK, 1) + acc_u[s + 1]
            ret[d, :, h * 128 : (h + 1) * 128] = jnp.where(low, even, odd).astype(bf16)
        return 0

    lax.fori_loop(0, PEERS, pack, 0, unroll=4)


def far(arrived, own, back, slot):
    return pl.pallas_call(
        far_kernel,
        out_shape=(
            jax.ShapeDtypeStruct((LEAVES, RHS, RANK), bf16),
            jax.ShapeDtypeStruct((PEERS, RHS, 256), bf16),
        ),
        in_specs=[VMEM] * 3 + [SMEM],
        out_specs=(VMEM,) * 2,
        scratch_shapes=[
            pltpu.VMEM((SLOTS, 16, 128), bf16),
            pltpu.VMEM((SLOTS, RHS, 128), bf16),
            pltpu.VMEM((16, FAR * RANK), bf16),
            pltpu.VMEM((16, FAR * RANK), bf16),
            pltpu.VMEM((RHS, FAR * RANK), bf16),
            pltpu.VMEM((RHS, FAR * RANK), bf16),
            pltpu.VMEM((RANK, FAR * RANK), bf16),
            pltpu.VMEM((RANK, FAR * RANK), bf16),
            pltpu.VMEM((SLOTS, RHS, 128), f32),
            pltpu.VMEM((SLOTS, RHS, 128), f32),
        ],
        compiler_params=params(),
        name="far",
    )(arrived, own, back, slot)


def post_kernel(came, send, near_out, far_in, row_basis, col_basis, product, adjoint, acc_l, acc_u):
    acc_l[...] = jnp.zeros_like(acc_l)
    acc_u[...] = jnp.zeros_like(acc_u)

    def peer(d, _):
        for h in range(2):
            tile = came[d, :, h * 128 : (h + 1) * 128].astype(f32)
            acc_l[send[2 * h, d]] += tile
            acc_u[send[2 * h + 1, d]] += tile
        return 0

    lax.fori_loop(0, PEERS, peer, 0, unroll=4)

    def leaf(j, _):
        total = (acc_l[j] + pltpu.roll(acc_u[j], RANK, 1))[:, :RANK].astype(bf16)
        adjoint[j] = near_out[j, RHS:, :] + jnp.dot(total, col_basis[j], preferred_element_type=f32)
        product[j] = near_out[j, :RHS, :] + jnp.dot(far_in[j], row_basis[j], preferred_element_type=f32)
        return 0

    lax.fori_loop(0, LEAVES, leaf, 0, unroll=4)


def post(came, send, near_out, far_in, row_basis, col_basis):
    return pl.pallas_call(
        post_kernel,
        out_shape=(jax.ShapeDtypeStruct((LEAVES, RHS, SIZE), f32),) * 2,
        in_specs=[VMEM, SMEM] + [VMEM] * 4,
        out_specs=(VMEM,) * 2,
        scratch_shapes=[pltpu.VMEM((LEAVES, RHS, 128), f32)] * 2,
        compiler_params=params(),
        name="post",
    )(came, send, near_out, far_in, row_basis, col_basis)


def local(probe, weights, points, skeleton, row_basis, col_basis, near_leaf, far_slot, send_leaf):
    send = send_leaf.transpose(0, 2, 1).reshape(CAP, PEERS)
    payload, back, own, block = prep(
        probe, weights, points.transpose(1, 0, 2), skeleton, row_basis, col_basis, near_leaf.T, send
    )
    near_part, arrived, halo = near_first(block, payload)
    far_in, ret = far(arrived, own, back, far_slot)
    near_out, came = near_rest(block, halo, near_part, ret)
    return post(came, send, near_out, far_in, row_basis, col_basis)


def solution(mesh):
    lead = P(("leaf", "sub"), None, None)
    flat = P(("leaf", "sub"), None)
    return jax.shard_map(
        local,
        mesh=mesh,
        in_specs=(lead, lead, lead, flat, lead, lead, flat, flat, lead),
        out_specs=(lead, lead),
        check_vma=False,
    )
```

```python
import functools

import jax
import jax.numpy as jnp
from jax import lax
from jax.experimental import pallas as pl
from jax.experimental.pallas import tpu as pltpu
from jax.sharding import PartitionSpec as P

REACH = 8
SCALE = 3.0**0.5 / 0.5
LOG2E = 1.4426950408889634
SOFTENING = 0.01
NUGGET = 0.5
LEAVES = 64
EXT = LEAVES + 2 * REACH
BAND = REACH + 1
RHS = 16
SIZE = 256
RANK = 64
CAP = 4
PREP_MIB = 54
PEERS = 128
SLOTS = PEERS * CAP
FAR = 64
bf16 = jnp.bfloat16
f32 = jnp.float32
NT = (((1,), (1,)), ((), ()))
MESH = pl.DeviceIdType.MESH
ROWS = 48
FIRST_COLUMNS = 40
VMEM = pl.BlockSpec(memory_space=pltpu.VMEM)
ANY = pl.BlockSpec(memory_space=pl.ANY)
HBM = pl.BlockSpec(memory_space=pltpu.HBM)
SMEM = pl.BlockSpec(memory_space=pltpu.SMEM)


def params(mib=24, **more):
    return pltpu.CompilerParams(vmem_limit_bytes=mib * 2**20, **more)


def device_id():
    return lax.axis_index("leaf") * 4 + lax.axis_index("sub")


def kappa(v):
    s = v * lax.rsqrt(v)
    return ((s * (0.5 * SCALE) + 0.5) * jnp.exp2(s * (-SCALE * LOG2E))).astype(bf16)


def split3(n):
    a = n.astype(bf16).astype(f32)
    b = (n - a).astype(bf16).astype(f32)
    return a, b, n - a - b


def stack_rows(rows, height, width):
    at = lax.broadcasted_iota(jnp.int32, (height, width), 0)
    out = jnp.zeros((height, width), f32)
    for r, value in enumerate(rows):
        out = jnp.where(at == r, value, out)
    return out


def point_features(xyz):
    x, y, z = xyz
    n = x * x + y * y + z * z
    one = jnp.ones_like(x)
    right = [x, y, z, *split3(n), one, one, one]
    left = [-2.0 * x, -2.0 * y, -2.0 * z, one, one, one, *split3(n + SOFTENING)]
    return left, right


def prep_kernel(
    probe_h, weights_h, points_h, skeleton_h, row_basis_h, col_basis_h, near_leaf_h, send_h, out, back, own, block,
    probe, weights, points, skeleton, row_basis, col_basis, near_leaf, send, coef_t, feat_t, sk, cnt, pts, sems
):
    far = (near_leaf_h, points_h, skeleton_h, probe_h, weights_h, col_basis_h, row_basis_h, send_h)
    here = (near_leaf, points, skeleton, probe, weights, col_basis, row_basis, send)
    copies = [pltpu.make_async_copy(f, h, sems.at[n]) for n, (f, h) in enumerate(zip(far, here))]
    for copy in copies:
        copy.start()
    for copy in copies[:3]:
        copy.wait()
    low = lax.broadcasted_iota(jnp.int32, (RHS, 128), 1) < RANK
    low8 = lax.broadcasted_iota(jnp.int32, (8, 128), 1) < RANK
    low64 = lax.broadcasted_iota(jnp.int32, (LEAVES, 128), 1) < RANK
    xy = skeleton[:, 0:128].astype(f32)
    yx = pltpu.roll(xy, RANK, 1)
    sk[0] = jnp.where(low64, xy, yx)
    sk[1] = jnp.where(low64, yx, xy)
    z = skeleton[:, 128:192].astype(f32)
    sk[2] = jnp.concatenate([z, z], axis=1)
    ids = device_id() * LEAVES + lax.broadcasted_iota(jnp.int32, (32, LEAVES), 1)
    offset = lax.broadcasted_iota(jnp.int32, (32, LEAVES), 0)
    total = jnp.zeros((32, LEAVES), f32)
    for m in range(near_leaf.shape[0]):
        total = total + jnp.where(near_leaf[m : m + 1, :] == ids + (offset - REACH), 1.0, 0.0)
    total = jnp.where(offset <= 2 * REACH, total, 0.0)
    total = jnp.concatenate([total, total], axis=1)
    cnt[...] = jnp.concatenate([total, jnp.zeros((96, 128), f32)], axis=0).T[0:LEAVES]
    for c in range(3):
        pts[c] = points[c].astype(f32)
    for copy in copies[3:]:
        copy.wait()

    def leaf(j, _):
        c = lax.dot_general(probe[j], col_basis[j], NT, preferred_element_type=f32)
        coef_t[j] = jnp.concatenate([c, c], axis=1).astype(bf16)
        back[j] = lax.dot_general(weights[j], row_basis[j], NT, preferred_element_type=f32).astype(bf16)
        left, right = point_features(tuple(sk[k, pl.ds(j, 1), :] for k in range(3)))
        feat_t[j] = stack_rows(right[:8], 8, 128)
        own[j] = stack_rows(left, 128, 128)[:, :RANK].T.astype(bf16)
        block[j, 0:16, :] = probe[j]
        block[j, 16:32, :] = weights[j]
        n = cnt[pl.ds(j, 1), :]
        rows = [*(pts[c, pl.ds(j, 1), :] for c in range(3)), jnp.concatenate([n, jnp.zeros((1, 128), f32)], axis=1)]
        block[j, 32:48, :] = stack_rows(rows, 16, SIZE).astype(bf16)
        return 0

    lax.fori_loop(0, LEAVES, leaf, 0, unroll=8)

    def peer(d, _):
        at = [send[q, d] for q in range(CAP)]
        for h in range(2):
            out[d, :, h * 128 : (h + 1) * 128] = jnp.where(low, coef_t[at[2 * h]], coef_t[at[2 * h + 1]])
        f = [jnp.where(low8, feat_t[at[2 * h]], feat_t[at[2 * h + 1]]) for h in range(2)]
        out[d, :, 256:384] = jnp.concatenate(f, axis=0).astype(bf16)
        return 0

    lax.fori_loop(0, PEERS, peer, 0, unroll=8)


def prep(*operands):
    return pl.pallas_call(
        prep_kernel,
        out_shape=(
            jax.ShapeDtypeStruct((PEERS, RHS, 384), bf16),
            jax.ShapeDtypeStruct((LEAVES, RHS, RANK), bf16),
            jax.ShapeDtypeStruct((LEAVES, RANK, 128), bf16),
            jax.ShapeDtypeStruct((LEAVES, ROWS, SIZE), bf16),
        ),
        in_specs=[HBM] * 8,
        out_specs=(VMEM,) * 4,
        scratch_shapes=[pltpu.VMEM(a.shape, a.dtype) for a in operands[:7]]
        + [
            pltpu.SMEM((CAP, PEERS), jnp.int32),
            pltpu.VMEM((LEAVES, RHS, 128), bf16),
            pltpu.VMEM((LEAVES, 8, 128), f32),
            pltpu.VMEM((3, LEAVES, 128), f32),
            pltpu.VMEM((LEAVES, 128), f32),
            pltpu.VMEM((3, LEAVES, SIZE), f32),
            pltpu.SemaphoreType.DMA((8,)),
        ],
        compiler_params=params(PREP_MIB),
        name="prep",
    )(*operands)


def greet(me):
    barrier = pltpu.get_barrier_semaphore()

    def one(k, _):
        peer = lax.rem(me + k, PEERS)
        pl.semaphore_signal(barrier, inc=1, device_id=(peer // 4, lax.rem(peer, 4)), device_id_type=MESH)
        return 0

    one(1, 0)
    lax.fori_loop(2, PEERS, one, 0, unroll=6)


def all_here():
    pl.semaphore_wait(pltpu.get_barrier_semaphore(), PEERS - 1)


def send_all(me, source, target, send_sem, recv_sem, own_sem):
    pltpu.make_async_copy(source.at[me], target.at[me], own_sem).start()

    def one(k, _):
        peer = lax.rem(me + k, PEERS)
        pltpu.make_async_remote_copy(
            src_ref=source.at[peer],
            dst_ref=target.at[me],
            send_sem=send_sem,
            recv_sem=recv_sem,
            device_id=(peer // 4, lax.rem(peer, 4)),
            device_id_type=MESH,
        ).start()
        return 0

    one(1, 0)
    lax.fori_loop(2, PEERS, one, 0, unroll=6)


def wait_all(me, source, target, send_sem, recv_sem, own_sem):
    pltpu.make_async_copy(source.at[me], target.at[me], own_sem).wait()
    most = pl.ds(0, PEERS - 1)
    pltpu.make_async_copy(source.at[most], source.at[most], send_sem).wait()
    pltpu.make_async_copy(target.at[most], target.at[most], recv_sem).wait()


class Near:
    def __init__(self, vec, cnt, acc, left_t, right_t, ks, kt, va):
        self.vec, self.cnt, self.acc, self.left_t, self.right_t = vec, cnt, acc, left_t, right_t
        self.ks, self.kt, self.va = ks, kt, va

    def features(self, j, tile):
        self.vec[j] = tile[0:32, :]
        rows = tile[32:48, :].astype(f32)
        left, right = point_features((rows[0:1], rows[1:2], rows[2:3]))
        self.right_t[j] = stack_rows(right, 16, SIZE).astype(bf16)
        self.left_t[j] = stack_rows(left, 128, SIZE).T.astype(bf16)
        self.cnt[j] = rows[3:4, 0:128]

    def make(self, j, at, b):
        v = jnp.dot(self.left_t[j - REACH + b, :, 0:16], self.right_t[j], preferred_element_type=f32)
        k = kappa(v)
        self.ks[at][b * SIZE : (b + 1) * SIZE, :] = k
        if b < REACH:
            self.kt[at][b * SIZE : (b + 1) * SIZE, :] = k.T

    def make_all(self, j, at):
        for b in range(BAND):
            self.make(j, at, b)

    def step(self, j, at, j_next=None):
        ks, kt, va, acc = self.ks[at], self.kt[at], self.va[at], self.acc
        vj = self.vec[j]
        cj = self.cnt[j]

        def spread(c, rows=RHS):
            c = jnp.broadcast_to(c, (rows, 128))
            return jnp.concatenate([c, c], axis=1)

        total = spread(cj[:, REACH : REACH + 1] * NUGGET, 2 * RHS) * vj.astype(f32)
        for b in range(BAND):
            i = j - REACH + b
            d = REACH - b
            ahead = spread(self.cnt[i][:, REACH + d : REACH + d + 1]).astype(bf16)
            behind = spread(cj[:, REACH - d : REACH - d + 1]).astype(bf16)
            vi = self.vec[i]
            cols = slice(b * SIZE, (b + 1) * SIZE)
            va[0:16, cols] = vi[0:16] * behind
            va[16:32, cols] = vi[16:32] * ahead
            if b < REACH:
                vb = jnp.concatenate([vj[0:16] * ahead, vj[16:32] * behind], axis=0)
                acc[i] += jnp.dot(vb, kt[cols, :], preferred_element_type=f32)
            if b % 3 == 2:
                cols = slice((b - 2) * SIZE, (b + 1) * SIZE)
                total = total + jnp.dot(va[:, cols], ks[cols, :], preferred_element_type=f32)
            if j_next is not None:
                self.make(j_next, 1 - at, b)
        acc[j] += total


NEAR_SCRATCH = [
    pltpu.VMEM((EXT, 2 * RHS, SIZE), bf16),
    pltpu.VMEM((EXT, 1, 128), f32),
    pltpu.VMEM((EXT, 2 * RHS, SIZE), f32),
    pltpu.VMEM((EXT, SIZE, 128), bf16),
    pltpu.VMEM((EXT, 16, SIZE), bf16),
    pltpu.VMEM((BAND * SIZE, SIZE), bf16),
    pltpu.VMEM((BAND * SIZE, SIZE), bf16),
    pltpu.VMEM((BAND * SIZE, SIZE), bf16),
    pltpu.VMEM((BAND * SIZE, SIZE), bf16),
    pltpu.VMEM((2 * RHS, BAND * SIZE), bf16),
    pltpu.VMEM((2 * RHS, BAND * SIZE), bf16),
]


def near_first_kernel(
    block, payload, block_far, out, arrived, halo, vec, cnt, acc, left_t, right_t, ks0, ks1, kt0, kt1, va0, va1,
    send_sem, recv_sem, own_sem, edge_send, edge_recv
):
    me = device_id()
    greet(me)
    near = Near(vec, cnt, acc, left_t, right_t, (ks0, ks1), (kt0, kt1), (va0, va1))
    acc[...] = jnp.zeros_like(acc)

    def first(j, _):
        near.features(j + REACH, block[j])
        return 0

    lax.fori_loop(0, REACH + FIRST_COLUMNS, first, 0, unroll=4)
    begin = 2 * REACH
    near.make_all(begin, 0)
    all_here()
    edges = []
    for side in range(2):
        peer = lax.rem(me + (1 if side == 0 else PEERS - 1), PEERS)
        rows = pl.ds(LEAVES - REACH, REACH) if side == 0 else pl.ds(0, REACH)
        edges.append(
            pltpu.make_async_remote_copy(
                src_ref=block_far.at[rows],
                dst_ref=halo.at[pl.ds(side * REACH, REACH)],
                send_sem=edge_send.at[side],
                recv_sem=edge_recv.at[side],
                device_id=(peer // 4, lax.rem(peer, 4)),
                device_id_type=MESH,
            )
        )
        edges[-1].start()
    send_all(me, payload, arrived, send_sem, recv_sem, own_sem)

    def body(g, _):
        j = begin + 2 * g
        near.step(j, 0, j + 1)
        near.step(j + 1, 1, j + 2)
        return 0

    lax.fori_loop(0, FIRST_COLUMNS // 2 - 1, body, 0)
    j = begin + FIRST_COLUMNS - 2
    near.step(j, 0, j + 1)
    near.step(j + 1, 1)
    out[...] = acc[REACH : REACH + LEAVES]
    for edge in edges:
        edge.wait()
    wait_all(me, payload, arrived, send_sem, recv_sem, own_sem)


def near_first(block, payload):
    return pl.pallas_call(
        near_first_kernel,
        out_shape=(
            jax.ShapeDtypeStruct((LEAVES, 2 * RHS, SIZE), f32),
            jax.ShapeDtypeStruct((PEERS, RHS, 384), bf16),
            jax.ShapeDtypeStruct((2 * REACH, ROWS, SIZE), bf16),
        ),
        in_specs=[VMEM, ANY, ANY],
        out_specs=(VMEM, ANY, ANY),
        scratch_shapes=NEAR_SCRATCH
        + [pltpu.SemaphoreType.DMA] * 3
        + [pltpu.SemaphoreType.DMA((2,)), pltpu.SemaphoreType.DMA((2,))],
        compiler_params=params(collective_id=0, has_side_effects=True),
        name="near_first",
    )(block, payload, block)


def near_rest_kernel(
    block, halo, before, ret, out, came, vec, cnt, acc, left_t, right_t, ks0, ks1, kt0, kt1, va0, va1,
    send_sem, recv_sem, own_sem
):
    me = device_id()
    greet(me)
    near = Near(vec, cnt, acc, left_t, right_t, (ks0, ks1), (kt0, kt1), (va0, va1))

    def edge(j, _):
        near.features(j, halo[j])
        near.features(j + LEAVES + REACH, halo[j + REACH])
        acc[j] = jnp.zeros((2 * RHS, SIZE), f32)
        acc[j + LEAVES + REACH] = jnp.zeros((2 * RHS, SIZE), f32)
        return 0

    lax.fori_loop(0, REACH, edge, 0, unroll=2)

    def keep(j, _):
        acc[j + REACH] = before[j]
        return 0

    lax.fori_loop(0, LEAVES, keep, 0, unroll=4)

    def first(n, _):
        j = jnp.where(n < REACH, n, n - REACH + FIRST_COLUMNS)
        near.features(j + REACH, block[j])
        return 0

    lax.fori_loop(0, REACH + LEAVES - FIRST_COLUMNS, first, 0, unroll=4)
    begin = 2 * REACH + FIRST_COLUMNS
    upper = EXT - begin
    columns = upper + REACH

    def column(n):
        return jnp.where(n < upper, begin + n, n - upper + REACH)

    near.make_all(begin, 0)
    all_here()
    send_all(me, ret, came, send_sem, recv_sem, own_sem)

    def body(g, _):
        near.step(column(2 * g), 0, column(2 * g + 1))
        near.step(column(2 * g + 1), 1, column(2 * g + 2))
        return 0

    lax.fori_loop(0, columns // 2 - 1, body, 0)
    near.step(column(columns - 2), 0, column(columns - 1))
    near.step(column(columns - 1), 1)
    out[...] = acc[REACH : REACH + LEAVES]
    wait_all(me, ret, came, send_sem, recv_sem, own_sem)


def near_rest(block, halo, before, ret):
    return pl.pallas_call(
        near_rest_kernel,
        out_shape=(
            jax.ShapeDtypeStruct((LEAVES, 2 * RHS, SIZE), f32),
            jax.ShapeDtypeStruct((PEERS, RHS, 256), bf16),
        ),
        in_specs=[VMEM, VMEM, VMEM, ANY],
        out_specs=(VMEM, ANY),
        scratch_shapes=NEAR_SCRATCH + [pltpu.SemaphoreType.DMA] * 3,
        compiler_params=params(collective_id=1, has_side_effects=True),
        name="near_rest",
    )(block, halo, before, ret)


def far_kernel(arrived, own, back, slot, far_in, ret, feat, coef, gt0, gt1, ct0, ct1, ks0, ks1, acc_l, acc_u):
    gt, ct, ks = (gt0, gt1), (ct0, ct1), (ks0, ks1)
    low = lax.broadcasted_iota(jnp.int32, (RHS, 128), 1) < RANK
    low8 = lax.broadcasted_iota(jnp.int32, (8, 128), 1) < RANK
    tail = jnp.where(lax.broadcasted_iota(jnp.int32, (8, 128), 0) == 0, 1.0, 0.0).astype(f32)

    def both(x, mask):
        y = pltpu.roll(x, RANK, 1)
        return jnp.where(mask, x, y), jnp.where(mask, y, x)

    def table(d, _):
        for h in range(2):
            c = both(arrived[d, :, h * 128 : (h + 1) * 128].astype(f32), low)
            f = both(arrived[d, :, 256:384].astype(f32)[h * 8 : (h + 1) * 8], low8)
            for q in range(2):
                coef[d * CAP + 2 * h + q] = c[q].astype(bf16)
                feat[d * CAP + 2 * h + q] = jnp.concatenate([f[q], tail], axis=0).astype(bf16)
        return 0

    lax.fori_loop(0, PEERS, table, 0, unroll=4)
    acc_l[...] = jnp.zeros_like(acc_l)
    acc_u[...] = jnp.zeros_like(acc_u)

    def gather(i, p, t):
        for m in range(2 * t, 2 * t + 2):
            lanes = slice(m * 128, (m + 1) * 128)
            a, b = slot[i, 2 * m], slot[i, 2 * m + 1]
            gt[p][:, lanes] = jnp.where(low, feat[a], feat[b])
            ct[p][:, lanes] = jnp.where(low, coef[a], coef[b])

    def make(i, p, t):
        lanes = slice(t * 256, (t + 1) * 256)
        ks[p][:, lanes] = kappa(jnp.dot(own[i, :, 0:16], gt[p][:, lanes], preferred_element_type=f32))

    def apply(i, p, t, w):
        lanes = slice(t * 256, (t + w) * 256)
        part = lax.dot_general(ct[p][:, lanes], ks[p][:, lanes], NT, preferred_element_type=f32)
        rt = jnp.dot(back[i], ks[p][:, lanes], preferred_element_type=f32)
        for m in range(2 * w):
            tile = rt[:, m * 128 : (m + 1) * 128]
            acc_l[slot[i, 4 * t + 2 * m]] += tile
            acc_u[slot[i, 4 * t + 2 * m + 1]] += tile
        return part

    TILES = 16
    W = 2

    def step(i_next, p_next, i, p):
        total = None
        for t in range(0, TILES, W):
            part = apply(i, p, t, W)
            total = part if total is None else total + part
            for u in range(t, t + W):
                gather(i_next, p_next, u)
                make(i_next, p_next, u)
        far_in[i] = total.astype(bf16)

    for t in range(TILES):
        gather(0, 0, t)
        make(0, 0, t)

    def pair(g, _):
        step(2 * g + 1, 1, 2 * g, 0)
        step(jnp.minimum(2 * g + 2, LEAVES - 1), 0, 2 * g + 1, 1)
        return 0

    lax.fori_loop(0, LEAVES // 2, pair, 0)

    def pack(d, _):
        for h in range(2):
            s = d * CAP + 2 * h
            here = jnp.where(low, acc_l[s], acc_u[s + 1])
            over = jnp.where(low, acc_l[s + 1], acc_u[s])
            ret[d, :, h * 128 : (h + 1) * 128] = (here + pltpu.roll(over, RANK, 1)).astype(bf16)
        return 0

    lax.fori_loop(0, PEERS, pack, 0, unroll=8)


def far(arrived, own, back, slot):
    return pl.pallas_call(
        far_kernel,
        out_shape=(
            jax.ShapeDtypeStruct((LEAVES, RHS, RANK), bf16),
            jax.ShapeDtypeStruct((PEERS, RHS, 256), bf16),
        ),
        in_specs=[VMEM] * 3 + [SMEM],
        out_specs=(VMEM,) * 2,
        scratch_shapes=[
            pltpu.VMEM((SLOTS, 16, 128), bf16),
            pltpu.VMEM((SLOTS, RHS, 128), bf16),
            pltpu.VMEM((16, FAR * RANK), bf16),
            pltpu.VMEM((16, FAR * RANK), bf16),
            pltpu.VMEM((RHS, FAR * RANK), bf16),
            pltpu.VMEM((RHS, FAR * RANK), bf16),
            pltpu.VMEM((RANK, FAR * RANK), bf16),
            pltpu.VMEM((RANK, FAR * RANK), bf16),
            pltpu.VMEM((SLOTS, RHS, 128), f32),
            pltpu.VMEM((SLOTS, RHS, 128), f32),
        ],
        compiler_params=params(),
        name="far",
    )(arrived, own, back, slot)


def post_kernel(came, send, near_out, far_in, row_basis, col_basis, product, adjoint, acc_l, acc_u):
    acc_l[...] = jnp.zeros_like(acc_l)
    acc_u[...] = jnp.zeros_like(acc_u)

    def peer(d, _):
        for h in range(2):
            tile = came[d, :, h * 128 : (h + 1) * 128].astype(f32)
            acc_l[send[2 * h, d]] += tile
            acc_u[send[2 * h + 1, d]] += tile
        return 0

    lax.fori_loop(0, PEERS, peer, 0, unroll=8)

    def leaf(j, _):
        total = (acc_l[j] + pltpu.roll(acc_u[j], RANK, 1))[:, :RANK].astype(bf16)
        adjoint[j] = near_out[j, RHS:, :] + jnp.dot(total, col_basis[j], preferred_element_type=f32)
        product[j] = near_out[j, :RHS, :] + jnp.dot(far_in[j], row_basis[j], preferred_element_type=f32)
        return 0

    lax.fori_loop(0, LEAVES, leaf, 0, unroll=8)


def post(came, send, near_out, far_in, row_basis, col_basis):
    return pl.pallas_call(
        post_kernel,
        out_shape=(jax.ShapeDtypeStruct((LEAVES, RHS, SIZE), f32),) * 2,
        in_specs=[VMEM, SMEM] + [VMEM] * 4,
        out_specs=(VMEM,) * 2,
        scratch_shapes=[pltpu.VMEM((LEAVES, RHS, 128), f32)] * 2,
        compiler_params=params(),
        name="post",
    )(came, send, near_out, far_in, row_basis, col_basis)


def local(probe, weights, points, skeleton, row_basis, col_basis, near_leaf, far_slot, send_leaf):
    send = send_leaf.transpose(0, 2, 1).reshape(CAP, PEERS)
    payload, back, own, block = prep(
        probe, weights, points.transpose(1, 0, 2), skeleton, row_basis, col_basis, near_leaf.T, send
    )
    near_part, arrived, halo = near_first(block, payload)
    far_in, ret = far(arrived, own, back, far_slot)
    near_out, came = near_rest(block, halo, near_part, ret)
    return post(came, send, near_out, far_in, row_basis, col_basis)


def solution(mesh):
    lead = P(("leaf", "sub"), None, None)
    flat = P(("leaf", "sub"), None)
    return jax.shard_map(
        local,
        mesh=mesh,
        in_specs=(lead, lead, lead, flat, lead, lead, flat, flat, lead),
        out_specs=(lead, lead),
        check_vma=False,
    )
```

```python
import functools

import jax
import jax.numpy as jnp
from jax import lax
from jax.experimental import pallas as pl
from jax.experimental.pallas import tpu as pltpu
from jax.sharding import PartitionSpec as P

REACH = 8
SCALE = 3.0**0.5 / 0.5
LOG2E = 1.4426950408889634
SOFTENING = 0.01
NUGGET = 0.5
LEAVES = 64
EXT = LEAVES + 2 * REACH
BAND = REACH + 1
RHS = 16
SIZE = 256
RANK = 64
CAP = 4
PREP_MIB = 54
PEERS = 128
SLOTS = PEERS * CAP
FAR = 64
bf16 = jnp.bfloat16
f32 = jnp.float32
NT = (((1,), (1,)), ((), ()))
MESH = pl.DeviceIdType.MESH
ROWS = 48
FIRST_COLUMNS = 40
LAG = 4
VMEM = pl.BlockSpec(memory_space=pltpu.VMEM)
ANY = pl.BlockSpec(memory_space=pl.ANY)
HBM = pl.BlockSpec(memory_space=pltpu.HBM)
SMEM = pl.BlockSpec(memory_space=pltpu.SMEM)


def params(mib=24, **more):
    return pltpu.CompilerParams(vmem_limit_bytes=mib * 2**20, **more)


def device_id():
    return lax.axis_index("leaf") * 4 + lax.axis_index("sub")


def kappa(v):
    s = v * lax.rsqrt(v)
    return ((s * (0.5 * SCALE) + 0.5) * jnp.exp2(s * (-SCALE * LOG2E))).astype(bf16)


def split3(n):
    a = n.astype(bf16).astype(f32)
    b = (n - a).astype(bf16).astype(f32)
    return a, b, n - a - b


def stack_rows(rows, height, width):
    at = lax.broadcasted_iota(jnp.int32, (height, width), 0)
    out = jnp.zeros((height, width), f32)
    for r, value in enumerate(rows):
        out = jnp.where(at == r, value, out)
    return out


def point_features(xyz):
    x, y, z = xyz
    n = x * x + y * y + z * z
    one = jnp.ones_like(x)
    right = [x, y, z, *split3(n), one, one, one]
    left = [-2.0 * x, -2.0 * y, -2.0 * z, one, one, one, *split3(n + SOFTENING)]
    return left, right


def prep_kernel(
    probe_h, weights_h, points_h, skeleton_h, row_basis_h, col_basis_h, near_leaf_h, send_h, out, back, own, block,
    probe, weights, points, skeleton, row_basis, col_basis, near_leaf, send, coef_t, feat_t, sk, cnt, pts, sems
):
    far = (near_leaf_h, points_h, skeleton_h, probe_h, weights_h, col_basis_h, row_basis_h, send_h)
    here = (near_leaf, points, skeleton, probe, weights, col_basis, row_basis, send)
    copies = [pltpu.make_async_copy(f, h, sems.at[n]) for n, (f, h) in enumerate(zip(far, here))]
    for copy in copies:
        copy.start()
    for copy in copies[:3]:
        copy.wait()
    low = lax.broadcasted_iota(jnp.int32, (RHS, 128), 1) < RANK
    low8 = lax.broadcasted_iota(jnp.int32, (8, 128), 1) < RANK
    low64 = lax.broadcasted_iota(jnp.int32, (LEAVES, 128), 1) < RANK
    xy = skeleton[:, 0:128].astype(f32)
    yx = pltpu.roll(xy, RANK, 1)
    sk[0] = jnp.where(low64, xy, yx)
    sk[1] = jnp.where(low64, yx, xy)
    z = skeleton[:, 128:192].astype(f32)
    sk[2] = jnp.concatenate([z, z], axis=1)
    ids = device_id() * LEAVES + lax.broadcasted_iota(jnp.int32, (32, LEAVES), 1)
    offset = lax.broadcasted_iota(jnp.int32, (32, LEAVES), 0)
    total = jnp.zeros((32, LEAVES), f32)
    for m in range(near_leaf.shape[0]):
        total = total + jnp.where(near_leaf[m : m + 1, :] == ids + (offset - REACH), 1.0, 0.0)
    total = jnp.where(offset <= 2 * REACH, total, 0.0)
    total = jnp.concatenate([total, total], axis=1)
    cnt[...] = jnp.concatenate([total, jnp.zeros((96, 128), f32)], axis=0).T[0:LEAVES]
    for c in range(3):
        pts[c] = points[c].astype(f32)
    for copy in copies[3:]:
        copy.wait()

    def leaf(j, _):
        c = lax.dot_general(probe[j], col_basis[j], NT, preferred_element_type=f32)
        coef_t[j] = jnp.concatenate([c, c], axis=1).astype(bf16)
        back[j] = lax.dot_general(weights[j], row_basis[j], NT, preferred_element_type=f32).astype(bf16)
        left, right = point_features(tuple(sk[k, pl.ds(j, 1), :] for k in range(3)))
        feat_t[j] = stack_rows(right[:8], 8, 128)
        own[j] = stack_rows(left, 128, 128)[:, :RANK].T.astype(bf16)
        block[j, 0:16, :] = probe[j]
        block[j, 16:32, :] = weights[j]
        n = cnt[pl.ds(j, 1), :]
        rows = [*(pts[c, pl.ds(j, 1), :] for c in range(3)), jnp.concatenate([n, jnp.zeros((1, 128), f32)], axis=1)]
        block[j, 32:48, :] = stack_rows(rows, 16, SIZE).astype(bf16)
        return 0

    lax.fori_loop(0, LEAVES, leaf, 0, unroll=8)

    def peer(d, _):
        at = [send[q, d] for q in range(CAP)]
        for h in range(2):
            out[d, :, h * 128 : (h + 1) * 128] = jnp.where(low, coef_t[at[2 * h]], coef_t[at[2 * h + 1]])
        f = [jnp.where(low8, feat_t[at[2 * h]], feat_t[at[2 * h + 1]]) for h in range(2)]
        out[d, :, 256:384] = jnp.concatenate(f, axis=0).astype(bf16)
        return 0

    lax.fori_loop(0, PEERS, peer, 0, unroll=8)


def prep(*operands):
    return pl.pallas_call(
        prep_kernel,
        out_shape=(
            jax.ShapeDtypeStruct((PEERS, RHS, 384), bf16),
            jax.ShapeDtypeStruct((LEAVES, RHS, RANK), bf16),
            jax.ShapeDtypeStruct((LEAVES, RANK, 128), bf16),
            jax.ShapeDtypeStruct((LEAVES, ROWS, SIZE), bf16),
        ),
        in_specs=[HBM] * 8,
        out_specs=(VMEM,) * 4,
        scratch_shapes=[pltpu.VMEM(a.shape, a.dtype) for a in operands[:7]]
        + [
            pltpu.SMEM((CAP, PEERS), jnp.int32),
            pltpu.VMEM((LEAVES, RHS, 128), bf16),
            pltpu.VMEM((LEAVES, 8, 128), f32),
            pltpu.VMEM((3, LEAVES, 128), f32),
            pltpu.VMEM((LEAVES, 128), f32),
            pltpu.VMEM((3, LEAVES, SIZE), f32),
            pltpu.SemaphoreType.DMA((8,)),
        ],
        compiler_params=params(PREP_MIB),
        name="prep",
    )(*operands)


def greet(me):
    barrier = pltpu.get_barrier_semaphore()

    def one(k, _):
        peer = lax.rem(me + k, PEERS)
        pl.semaphore_signal(barrier, inc=1, device_id=(peer // 4, lax.rem(peer, 4)), device_id_type=MESH)
        return 0

    one(1, 0)
    lax.fori_loop(2, PEERS, one, 0, unroll=6)


def all_here():
    pl.semaphore_wait(pltpu.get_barrier_semaphore(), PEERS - 1)


def send_all(me, source, target, send_sem, recv_sem, own_sem):
    pltpu.make_async_copy(source.at[me], target.at[me], own_sem).start()

    def one(k, _):
        peer = lax.rem(me + k, PEERS)
        pltpu.make_async_remote_copy(
            src_ref=source.at[peer],
            dst_ref=target.at[me],
            send_sem=send_sem,
            recv_sem=recv_sem,
            device_id=(peer // 4, lax.rem(peer, 4)),
            device_id_type=MESH,
        ).start()
        return 0

    one(1, 0)
    lax.fori_loop(2, PEERS, one, 0, unroll=6)


def wait_all(me, source, target, send_sem, recv_sem, own_sem):
    pltpu.make_async_copy(source.at[me], target.at[me], own_sem).wait()
    most = pl.ds(0, PEERS - 1)
    pltpu.make_async_copy(source.at[most], source.at[most], send_sem).wait()
    pltpu.make_async_copy(target.at[most], target.at[most], recv_sem).wait()


class Near:
    def __init__(self, vec, cnt, acc, left_t, right_t, ks, kt, va):
        self.vec, self.cnt, self.acc, self.left_t, self.right_t = vec, cnt, acc, left_t, right_t
        self.ks, self.kt, self.va = ks, kt, va

    def features(self, j, tile):
        self.vec[j] = tile[0:32, :]
        rows = tile[32:48, :].astype(f32)
        left, right = point_features((rows[0:1], rows[1:2], rows[2:3]))
        self.right_t[j] = stack_rows(right, 16, SIZE).astype(bf16)
        self.left_t[j] = stack_rows(left, 128, SIZE).T.astype(bf16)
        self.cnt[j] = rows[3:4, 0:128]

    def make(self, j, at, b):
        v = jnp.dot(self.left_t[j - REACH + b, :, 0:16], self.right_t[j], preferred_element_type=f32)
        k = kappa(v)
        self.ks[at][b * SIZE : (b + 1) * SIZE, :] = k
        if b < REACH:
            self.kt[at][b * SIZE : (b + 1) * SIZE, :] = k.T

    def make_all(self, j, at):
        for b in range(BAND):
            self.make(j, at, b)

    def step(self, j, at, j_next=None):
        ks, kt, va, acc = self.ks[at], self.kt[at], self.va[at], self.acc
        vj = self.vec[j]
        cj = self.cnt[j]

        def spread(c, rows=RHS):
            c = jnp.broadcast_to(c, (rows, 128))
            return jnp.concatenate([c, c], axis=1)

        total = spread(cj[:, REACH : REACH + 1] * NUGGET, 2 * RHS) * vj.astype(f32)
        for b in range(BAND):
            i = j - REACH + b
            d = REACH - b
            ahead = spread(self.cnt[i][:, REACH + d : REACH + d + 1]).astype(bf16)
            behind = spread(cj[:, REACH - d : REACH - d + 1]).astype(bf16)
            vi = self.vec[i]
            cols = slice(b * SIZE, (b + 1) * SIZE)
            va[0:16, cols] = vi[0:16] * behind
            va[16:32, cols] = vi[16:32] * ahead
            if b < REACH:
                vb = jnp.concatenate([vj[0:16] * ahead, vj[16:32] * behind], axis=0)
                acc[i] += jnp.dot(vb, kt[cols, :], preferred_element_type=f32)
            if b % 3 == 2:
                cols = slice((b - 2) * SIZE, (b + 1) * SIZE)
                total = total + jnp.dot(va[:, cols], ks[cols, :], preferred_element_type=f32)
            if j_next is not None:
                self.make(j_next, 1 - at, b)
        acc[j] += total


    def upper_edge(self, g):
        lane = lax.broadcasted_iota(jnp.int32, (1, 128), 1)
        kt, acc = self.kt[0], self.acc

        def pick(row, at):
            c = jnp.sum(jnp.where(lane == at, row, 0.0), axis=1, keepdims=True)
            c = jnp.broadcast_to(c, (RHS, 128))
            return jnp.concatenate([c, c], axis=1).astype(bf16)

        def make(b, i, j):
            v = jnp.dot(self.left_t[i, :, 0:16], self.right_t[j], preferred_element_type=f32)
            kt[b * SIZE : (b + 1) * SIZE, :] = kappa(v).T

        def apply(b, i, j, d):
            ahead = pick(self.cnt[i], REACH + d)
            behind = pick(self.cnt[j], REACH - d)
            vj = self.vec[j]
            vb = jnp.concatenate([vj[0:16] * ahead, vj[16:32] * behind], axis=0)
            acc[i] += jnp.dot(vb, kt[b * SIZE : (b + 1) * SIZE, :], preferred_element_type=f32)

        pairs = []
        for b in range(BAND + LAG):
            if b < BAND:
                one = b < REACH - g
                i = jnp.where(one, LEAVES + g + b, LEAVES + b - 1)
                j = jnp.where(one, LEAVES + REACH + g, EXT - 1 - g)
                pairs.append((i, j, jnp.where(one, REACH - b, 2 * REACH - b - g)))
                make(b, i, j)
            if b >= LAG:
                apply(b - LAG, *pairs[b - LAG])


NEAR_SCRATCH = [
    pltpu.VMEM((EXT, 2 * RHS, SIZE), bf16),
    pltpu.VMEM((EXT, 1, 128), f32),
    pltpu.VMEM((EXT, 2 * RHS, SIZE), f32),
    pltpu.VMEM((EXT, SIZE, 128), bf16),
    pltpu.VMEM((EXT, 16, SIZE), bf16),
    pltpu.VMEM((BAND * SIZE, SIZE), bf16),
    pltpu.VMEM((BAND * SIZE, SIZE), bf16),
    pltpu.VMEM((BAND * SIZE, SIZE), bf16),
    pltpu.VMEM((BAND * SIZE, SIZE), bf16),
    pltpu.VMEM((2 * RHS, BAND * SIZE), bf16),
    pltpu.VMEM((2 * RHS, BAND * SIZE), bf16),
]


def near_first_kernel(
    block, payload, block_far, out, arrived, halo, vec, cnt, acc, left_t, right_t, ks0, ks1, kt0, kt1, va0, va1,
    send_sem, recv_sem, own_sem, edge_send, edge_recv
):
    me = device_id()
    greet(me)
    near = Near(vec, cnt, acc, left_t, right_t, (ks0, ks1), (kt0, kt1), (va0, va1))
    acc[...] = jnp.zeros_like(acc)

    def first(j, _):
        near.features(j + REACH, block[j])
        return 0

    lax.fori_loop(0, REACH + FIRST_COLUMNS, first, 0, unroll=4)
    begin = 2 * REACH
    near.make_all(begin, 0)
    all_here()
    edges = []
    for side in range(2):
        peer = lax.rem(me + (1 if side == 0 else PEERS - 1), PEERS)
        rows = pl.ds(LEAVES - REACH, REACH) if side == 0 else pl.ds(0, REACH)
        edges.append(
            pltpu.make_async_remote_copy(
                src_ref=block_far.at[rows],
                dst_ref=halo.at[pl.ds(side * REACH, REACH)],
                send_sem=edge_send.at[side],
                recv_sem=edge_recv.at[side],
                device_id=(peer // 4, lax.rem(peer, 4)),
                device_id_type=MESH,
            )
        )
        edges[-1].start()
    send_all(me, payload, arrived, send_sem, recv_sem, own_sem)

    def body(g, _):
        j = begin + 2 * g
        near.step(j, 0, j + 1)
        near.step(j + 1, 1, j + 2)
        return 0

    lax.fori_loop(0, FIRST_COLUMNS // 2 - 1, body, 0)
    j = begin + FIRST_COLUMNS - 2
    near.step(j, 0, j + 1)
    near.step(j + 1, 1)
    out[...] = acc[REACH : REACH + LEAVES]
    for edge in edges:
        edge.wait()
    wait_all(me, payload, arrived, send_sem, recv_sem, own_sem)


def near_first(block, payload):
    return pl.pallas_call(
        near_first_kernel,
        out_shape=(
            jax.ShapeDtypeStruct((LEAVES, 2 * RHS, SIZE), f32),
            jax.ShapeDtypeStruct((PEERS, RHS, 384), bf16),
            jax.ShapeDtypeStruct((2 * REACH, ROWS, SIZE), bf16),
        ),
        in_specs=[VMEM, ANY, ANY],
        out_specs=(VMEM, ANY, ANY),
        scratch_shapes=NEAR_SCRATCH
        + [pltpu.SemaphoreType.DMA] * 3
        + [pltpu.SemaphoreType.DMA((2,)), pltpu.SemaphoreType.DMA((2,))],
        compiler_params=params(collective_id=0, has_side_effects=True),
        name="near_first",
    )(block, payload, block)


def near_rest_kernel(
    block, halo, before, ret, out, came, vec, cnt, acc, left_t, right_t, ks0, ks1, kt0, kt1, va0, va1,
    send_sem, recv_sem, own_sem
):
    me = device_id()
    greet(me)
    near = Near(vec, cnt, acc, left_t, right_t, (ks0, ks1), (kt0, kt1), (va0, va1))

    def edge(j, _):
        near.features(j, halo[j])
        near.features(j + LEAVES + REACH, halo[j + REACH])
        acc[j] = jnp.zeros((2 * RHS, SIZE), f32)
        acc[j + LEAVES + REACH] = jnp.zeros((2 * RHS, SIZE), f32)
        return 0

    lax.fori_loop(0, REACH, edge, 0, unroll=2)

    def keep(j, _):
        acc[j + REACH] = before[j]
        return 0

    lax.fori_loop(0, LEAVES, keep, 0, unroll=4)

    def first(n, _):
        j = jnp.where(n < REACH, n, n - REACH + FIRST_COLUMNS)
        near.features(j + REACH, block[j])
        return 0

    lax.fori_loop(0, REACH + LEAVES - FIRST_COLUMNS, first, 0, unroll=4)
    begin = 2 * REACH + FIRST_COLUMNS
    upper = LEAVES + REACH - begin
    columns = upper + REACH

    def column(n):
        return jnp.where(n < upper, begin + n, n - upper + REACH)

    near.make_all(begin, 0)
    all_here()
    send_all(me, ret, came, send_sem, recv_sem, own_sem)

    def body(g, _):
        near.step(column(2 * g), 0, column(2 * g + 1))
        near.step(column(2 * g + 1), 1, column(2 * g + 2))
        return 0

    lax.fori_loop(0, columns // 2 - 1, body, 0)
    near.step(column(columns - 2), 0, column(columns - 1))
    near.step(column(columns - 1), 1)

    def last(g, _):
        near.upper_edge(g)
        return 0

    lax.fori_loop(0, REACH // 2, last, 0)
    out[...] = acc[REACH : REACH + LEAVES]
    wait_all(me, ret, came, send_sem, recv_sem, own_sem)


def near_rest(block, halo, before, ret):
    return pl.pallas_call(
        near_rest_kernel,
        out_shape=(
            jax.ShapeDtypeStruct((LEAVES, 2 * RHS, SIZE), f32),
            jax.ShapeDtypeStruct((PEERS, RHS, 256), bf16),
        ),
        in_specs=[VMEM, VMEM, VMEM, ANY],
        out_specs=(VMEM, ANY),
        scratch_shapes=NEAR_SCRATCH + [pltpu.SemaphoreType.DMA] * 3,
        compiler_params=params(collective_id=1, has_side_effects=True),
        name="near_rest",
    )(block, halo, before, ret)


def far_kernel(arrived, own, back, slot, far_in, ret, feat, coef, gt0, gt1, ct0, ct1, ks0, ks1, acc_l, acc_u):
    gt, ct, ks = (gt0, gt1), (ct0, ct1), (ks0, ks1)
    low = lax.broadcasted_iota(jnp.int32, (RHS, 128), 1) < RANK
    low8 = lax.broadcasted_iota(jnp.int32, (8, 128), 1) < RANK
    tail = jnp.where(lax.broadcasted_iota(jnp.int32, (8, 128), 0) == 0, 1.0, 0.0).astype(f32)

    def both(x, mask):
        y = pltpu.roll(x, RANK, 1)
        return jnp.where(mask, x, y), jnp.where(mask, y, x)

    def table(d, _):
        for h in range(2):
            c = both(arrived[d, :, h * 128 : (h + 1) * 128].astype(f32), low)
            f = both(arrived[d, :, 256:384].astype(f32)[h * 8 : (h + 1) * 8], low8)
            for q in range(2):
                coef[d * CAP + 2 * h + q] = c[q].astype(bf16)
                feat[d * CAP + 2 * h + q] = jnp.concatenate([f[q], tail], axis=0).astype(bf16)
        return 0

    lax.fori_loop(0, PEERS, table, 0, unroll=4)
    acc_l[...] = jnp.zeros_like(acc_l)
    acc_u[...] = jnp.zeros_like(acc_u)

    def gather(i, p, t):
        for m in range(2 * t, 2 * t + 2):
            lanes = slice(m * 128, (m + 1) * 128)
            a, b = slot[i, 2 * m], slot[i, 2 * m + 1]
            gt[p][:, lanes] = jnp.where(low, feat[a], feat[b])
            ct[p][:, lanes] = jnp.where(low, coef[a], coef[b])

    def make(i, p, t):
        lanes = slice(t * 256, (t + 1) * 256)
        ks[p][:, lanes] = kappa(jnp.dot(own[i, :, 0:16], gt[p][:, lanes], preferred_element_type=f32))

    def apply(i, p, t, w):
        lanes = slice(t * 256, (t + w) * 256)
        part = lax.dot_general(ct[p][:, lanes], ks[p][:, lanes], NT, preferred_element_type=f32)
        rt = jnp.dot(back[i], ks[p][:, lanes], preferred_element_type=f32)
        for m in range(2 * w):
            tile = rt[:, m * 128 : (m + 1) * 128]
            acc_l[slot[i, 4 * t + 2 * m]] += tile
            acc_u[slot[i, 4 * t + 2 * m + 1]] += tile
        return part

    TILES = 16
    W = 2

    def step(i_next, p_next, i, p):
        total = None
        for t in range(0, TILES, W):
            part = apply(i, p, t, W)
            total = part if total is None else total + part
            for u in range(t, t + W):
                gather(i_next, p_next, u)
                make(i_next, p_next, u)
        far_in[i] = total.astype(bf16)

    for t in range(TILES):
        gather(0, 0, t)
        make(0, 0, t)

    def pair(g, _):
        step(2 * g + 1, 1, 2 * g, 0)
        step(jnp.minimum(2 * g + 2, LEAVES - 1), 0, 2 * g + 1, 1)
        return 0

    lax.fori_loop(0, LEAVES // 2, pair, 0)

    def pack(d, _):
        for h in range(2):
            s = d * CAP + 2 * h
            here = jnp.where(low, acc_l[s], acc_u[s + 1])
            over = jnp.where(low, acc_l[s + 1], acc_u[s])
            ret[d, :, h * 128 : (h + 1) * 128] = (here + pltpu.roll(over, RANK, 1)).astype(bf16)
        return 0

    lax.fori_loop(0, PEERS, pack, 0, unroll=8)


def far(arrived, own, back, slot):
    return pl.pallas_call(
        far_kernel,
        out_shape=(
            jax.ShapeDtypeStruct((LEAVES, RHS, RANK), bf16),
            jax.ShapeDtypeStruct((PEERS, RHS, 256), bf16),
        ),
        in_specs=[VMEM] * 3 + [SMEM],
        out_specs=(VMEM,) * 2,
        scratch_shapes=[
            pltpu.VMEM((SLOTS, 16, 128), bf16),
            pltpu.VMEM((SLOTS, RHS, 128), bf16),
            pltpu.VMEM((16, FAR * RANK), bf16),
            pltpu.VMEM((16, FAR * RANK), bf16),
            pltpu.VMEM((RHS, FAR * RANK), bf16),
            pltpu.VMEM((RHS, FAR * RANK), bf16),
            pltpu.VMEM((RANK, FAR * RANK), bf16),
            pltpu.VMEM((RANK, FAR * RANK), bf16),
            pltpu.VMEM((SLOTS, RHS, 128), f32),
            pltpu.VMEM((SLOTS, RHS, 128), f32),
        ],
        compiler_params=params(),
        name="far",
    )(arrived, own, back, slot)


def post_kernel(came, send, near_out, far_in, row_basis, col_basis, product, adjoint, acc_l, acc_u):
    acc_l[...] = jnp.zeros_like(acc_l)
    acc_u[...] = jnp.zeros_like(acc_u)

    def peer(d, _):
        for h in range(2):
            tile = came[d, :, h * 128 : (h + 1) * 128].astype(f32)
            acc_l[send[2 * h, d]] += tile
            acc_u[send[2 * h + 1, d]] += tile
        return 0

    lax.fori_loop(0, PEERS, peer, 0, unroll=8)

    def leaf(j, _):
        total = (acc_l[j] + pltpu.roll(acc_u[j], RANK, 1))[:, :RANK].astype(bf16)
        adjoint[j] = near_out[j, RHS:, :] + jnp.dot(total, col_basis[j], preferred_element_type=f32)
        product[j] = near_out[j, :RHS, :] + jnp.dot(far_in[j], row_basis[j], preferred_element_type=f32)
        return 0

    lax.fori_loop(0, LEAVES, leaf, 0, unroll=8)


def post(came, send, near_out, far_in, row_basis, col_basis):
    return pl.pallas_call(
        post_kernel,
        out_shape=(jax.ShapeDtypeStruct((LEAVES, RHS, SIZE), f32),) * 2,
        in_specs=[VMEM, SMEM] + [VMEM] * 4,
        out_specs=(VMEM,) * 2,
        scratch_shapes=[pltpu.VMEM((LEAVES, RHS, 128), f32)] * 2,
        compiler_params=params(),
        name="post",
    )(came, send, near_out, far_in, row_basis, col_basis)


def local(probe, weights, points, skeleton, row_basis, col_basis, near_leaf, far_slot, send_leaf):
    send = send_leaf.transpose(0, 2, 1).reshape(CAP, PEERS)
    payload, back, own, block = prep(
        probe, weights, points.transpose(1, 0, 2), skeleton, row_basis, col_basis, near_leaf.T, send
    )
    near_part, arrived, halo = near_first(block, payload)
    far_in, ret = far(arrived, own, back, far_slot)
    near_out, came = near_rest(block, halo, near_part, ret)
    return post(came, send, near_out, far_in, row_basis, col_basis)


def solution(mesh):
    lead = P(("leaf", "sub"), None, None)
    flat = P(("leaf", "sub"), None)
    return jax.shard_map(
        local,
        mesh=mesh,
        in_specs=(lead, lead, lead, flat, lead, lead, flat, flat, lead),
        out_specs=(lead, lead),
        check_vma=False,
    )
```

```python
import functools

import jax
import jax.numpy as jnp
from jax import lax
from jax.experimental import pallas as pl
from jax.experimental.pallas import tpu as pltpu
from jax.sharding import PartitionSpec as P

REACH = 8
SCALE = 3.0**0.5 / 0.5
LOG2E = 1.4426950408889634
SOFTENING = 0.01
NUGGET = 0.5
LEAVES = 64
EXT = LEAVES + 2 * REACH
BAND = REACH + 1
RHS = 16
SIZE = 256
RANK = 64
CAP = 4
PREP_MIB = 54
PEERS = 128
SLOTS = PEERS * CAP
FAR = 64
bf16 = jnp.bfloat16
f32 = jnp.float32
NT = (((1,), (1,)), ((), ()))
MESH = pl.DeviceIdType.MESH
ROWS = 48
FIRST_COLUMNS = 40
LAG = 4
VMEM = pl.BlockSpec(memory_space=pltpu.VMEM)
ANY = pl.BlockSpec(memory_space=pl.ANY)
HBM = pl.BlockSpec(memory_space=pltpu.HBM)
SMEM = pl.BlockSpec(memory_space=pltpu.SMEM)


def params(mib=24, **more):
    return pltpu.CompilerParams(vmem_limit_bytes=mib * 2**20, **more)


def device_id():
    return lax.axis_index("leaf") * 4 + lax.axis_index("sub")


def kappa(v):
    z = (v * lax.rsqrt(v) * (-SCALE * LOG2E)).astype(bf16)
    return (bf16(0.5) - z * bf16(0.5 / LOG2E)) * jnp.exp2(z)


def split3(n):
    a = n.astype(bf16).astype(f32)
    b = (n - a).astype(bf16).astype(f32)
    return a, b, n - a - b


def stack_rows(rows, height, width):
    at = lax.broadcasted_iota(jnp.int32, (height, width), 0)
    out = jnp.zeros((height, width), f32)
    for r, value in enumerate(rows):
        out = jnp.where(at == r, value, out)
    return out


def point_features(xyz):
    x, y, z = xyz
    n = x * x + y * y + z * z
    one = jnp.ones_like(x)
    right = [x, y, z, *split3(n), one, one, one]
    left = [-2.0 * x, -2.0 * y, -2.0 * z, one, one, one, *split3(n + SOFTENING)]
    return left, right


def prep_kernel(
    probe_h, weights_h, points_h, skeleton_h, row_basis_h, col_basis_h, near_leaf_h, send_h, out, back, own, block,
    probe, weights, points, skeleton, row_basis, col_basis, near_leaf, send, coef_t, feat_t, sk, cnt, pts, sems
):
    far = (near_leaf_h, points_h, skeleton_h, probe_h, weights_h, col_basis_h, row_basis_h, send_h)
    here = (near_leaf, points, skeleton, probe, weights, col_basis, row_basis, send)
    copies = [pltpu.make_async_copy(f, h, sems.at[n]) for n, (f, h) in enumerate(zip(far, here))]
    for copy in copies:
        copy.start()
    for copy in copies[:3]:
        copy.wait()
    low = lax.broadcasted_iota(jnp.int32, (RHS, 128), 1) < RANK
    low8 = lax.broadcasted_iota(jnp.int32, (8, 128), 1) < RANK
    low64 = lax.broadcasted_iota(jnp.int32, (LEAVES, 128), 1) < RANK
    xy = skeleton[:, 0:128].astype(f32)
    yx = pltpu.roll(xy, RANK, 1)
    sk[0] = jnp.where(low64, xy, yx)
    sk[1] = jnp.where(low64, yx, xy)
    z = skeleton[:, 128:192].astype(f32)
    sk[2] = jnp.concatenate([z, z], axis=1)
    ids = device_id() * LEAVES + lax.broadcasted_iota(jnp.int32, (32, LEAVES), 1)
    offset = lax.broadcasted_iota(jnp.int32, (32, LEAVES), 0)
    total = jnp.zeros((32, LEAVES), f32)
    for m in range(near_leaf.shape[0]):
        total = total + jnp.where(near_leaf[m : m + 1, :] == ids + (offset - REACH), 1.0, 0.0)
    total = jnp.where(offset <= 2 * REACH, total, 0.0)
    total = jnp.concatenate([total, total], axis=1)
    cnt[...] = jnp.concatenate([total, jnp.zeros((96, 128), f32)], axis=0).T[0:LEAVES]
    for c in range(3):
        pts[c] = points[c].astype(f32)
    for copy in copies[3:]:
        copy.wait()

    def leaf(j, _):
        c = lax.dot_general(probe[j], col_basis[j], NT, preferred_element_type=f32)
        coef_t[j] = jnp.concatenate([c, c], axis=1).astype(bf16)
        back[j] = lax.dot_general(weights[j], row_basis[j], NT, preferred_element_type=f32).astype(bf16)
        left, right = point_features(tuple(sk[k, pl.ds(j, 1), :] for k in range(3)))
        feat_t[j] = stack_rows(right[:8], 8, 128)
        own[j] = stack_rows(left, 128, 128)[:, :RANK].T.astype(bf16)
        block[j, 0:16, :] = probe[j]
        block[j, 16:32, :] = weights[j]
        n = cnt[pl.ds(j, 1), :]
        rows = [*(pts[c, pl.ds(j, 1), :] for c in range(3)), jnp.concatenate([n, jnp.zeros((1, 128), f32)], axis=1)]
        block[j, 32:48, :] = stack_rows(rows, 16, SIZE).astype(bf16)
        return 0

    lax.fori_loop(0, LEAVES, leaf, 0, unroll=8)

    def peer(d, _):
        at = [send[q, d] for q in range(CAP)]
        for h in range(2):
            out[d, :, h * 128 : (h + 1) * 128] = jnp.where(low, coef_t[at[2 * h]], coef_t[at[2 * h + 1]])
        f = [jnp.where(low8, feat_t[at[2 * h]], feat_t[at[2 * h + 1]]) for h in range(2)]
        out[d, :, 256:384] = jnp.concatenate(f, axis=0).astype(bf16)
        return 0

    lax.fori_loop(0, PEERS, peer, 0, unroll=8)


def prep(*operands):
    return pl.pallas_call(
        prep_kernel,
        out_shape=(
            jax.ShapeDtypeStruct((PEERS, RHS, 384), bf16),
            jax.ShapeDtypeStruct((LEAVES, RHS, RANK), bf16),
            jax.ShapeDtypeStruct((LEAVES, RANK, 128), bf16),
            jax.ShapeDtypeStruct((LEAVES, ROWS, SIZE), bf16),
        ),
        in_specs=[HBM] * 8,
        out_specs=(VMEM,) * 4,
        scratch_shapes=[pltpu.VMEM(a.shape, a.dtype) for a in operands[:7]]
        + [
            pltpu.SMEM((CAP, PEERS), jnp.int32),
            pltpu.VMEM((LEAVES, RHS, 128), bf16),
            pltpu.VMEM((LEAVES, 8, 128), f32),
            pltpu.VMEM((3, LEAVES, 128), f32),
            pltpu.VMEM((LEAVES, 128), f32),
            pltpu.VMEM((3, LEAVES, SIZE), f32),
            pltpu.SemaphoreType.DMA((8,)),
        ],
        compiler_params=params(PREP_MIB),
        name="prep",
    )(*operands)


def greet(me):
    barrier = pltpu.get_barrier_semaphore()

    def one(k, _):
        peer = lax.rem(me + k, PEERS)
        pl.semaphore_signal(barrier, inc=1, device_id=(peer // 4, lax.rem(peer, 4)), device_id_type=MESH)
        return 0

    one(1, 0)
    lax.fori_loop(2, PEERS, one, 0, unroll=6)


def all_here():
    pl.semaphore_wait(pltpu.get_barrier_semaphore(), PEERS - 1)


def send_all(me, source, target, send_sem, recv_sem, own_sem):
    pltpu.make_async_copy(source.at[me], target.at[me], own_sem).start()

    def one(k, _):
        peer = lax.rem(me + k, PEERS)
        pltpu.make_async_remote_copy(
            src_ref=source.at[peer],
            dst_ref=target.at[me],
            send_sem=send_sem,
            recv_sem=recv_sem,
            device_id=(peer // 4, lax.rem(peer, 4)),
            device_id_type=MESH,
        ).start()
        return 0

    one(1, 0)
    lax.fori_loop(2, PEERS, one, 0, unroll=6)


def wait_all(me, source, target, send_sem, recv_sem, own_sem):
    pltpu.make_async_copy(source.at[me], target.at[me], own_sem).wait()
    most = pl.ds(0, PEERS - 1)
    pltpu.make_async_copy(source.at[most], source.at[most], send_sem).wait()
    pltpu.make_async_copy(target.at[most], target.at[most], recv_sem).wait()


class Near:
    def __init__(self, vec, cnt, acc, left_t, right_t, ks, kt, va):
        self.vec, self.cnt, self.acc, self.left_t, self.right_t = vec, cnt, acc, left_t, right_t
        self.ks, self.kt, self.va = ks, kt, va

    def features(self, j, tile):
        self.vec[j] = tile[0:32, :]
        rows = tile[32:48, :].astype(f32)
        left, right = point_features((rows[0:1], rows[1:2], rows[2:3]))
        self.right_t[j] = stack_rows(right, 16, SIZE).astype(bf16)
        self.left_t[j] = stack_rows(left, 128, SIZE).T.astype(bf16)
        self.cnt[j] = rows[3:4, 0:128]

    def make(self, j, at, b):
        v = jnp.dot(self.left_t[j - REACH + b, :, 0:16], self.right_t[j], preferred_element_type=f32)
        k = kappa(v)
        self.ks[at][b * SIZE : (b + 1) * SIZE, :] = k
        if b < REACH:
            self.kt[at][b * SIZE : (b + 1) * SIZE, :] = k.T

    def make_all(self, j, at):
        for b in range(BAND):
            self.make(j, at, b)

    def step(self, j, at, j_next=None):
        ks, kt, va, acc = self.ks[at], self.kt[at], self.va[at], self.acc
        vj = self.vec[j]
        cj = self.cnt[j]

        def spread(c, rows=RHS):
            c = jnp.broadcast_to(c, (rows, 128))
            return jnp.concatenate([c, c], axis=1)

        total = spread(cj[:, REACH : REACH + 1] * NUGGET, 2 * RHS) * vj.astype(f32)
        for b in range(BAND):
            i = j - REACH + b
            d = REACH - b
            ahead = spread(self.cnt[i][:, REACH + d : REACH + d + 1]).astype(bf16)
            behind = spread(cj[:, REACH - d : REACH - d + 1]).astype(bf16)
            vi = self.vec[i]
            cols = slice(b * SIZE, (b + 1) * SIZE)
            va[0:16, cols] = vi[0:16] * behind
            va[16:32, cols] = vi[16:32] * ahead
            if b < REACH:
                vb = jnp.concatenate([vj[0:16] * ahead, vj[16:32] * behind], axis=0)
                acc[i] += jnp.dot(vb, kt[cols, :], preferred_element_type=f32)
            if b % 3 == 2:
                cols = slice((b - 2) * SIZE, (b + 1) * SIZE)
                total = total + jnp.dot(va[:, cols], ks[cols, :], preferred_element_type=f32)
            if j_next is not None:
                self.make(j_next, 1 - at, b)
        acc[j] += total


    def upper_edge(self, g):
        lane = lax.broadcasted_iota(jnp.int32, (1, 128), 1)
        kt, acc = self.kt[0], self.acc

        def pick(row, at):
            c = jnp.sum(jnp.where(lane == at, row, 0.0), axis=1, keepdims=True)
            c = jnp.broadcast_to(c, (RHS, 128))
            return jnp.concatenate([c, c], axis=1).astype(bf16)

        def make(b, i, j):
            v = jnp.dot(self.left_t[i, :, 0:16], self.right_t[j], preferred_element_type=f32)
            kt[b * SIZE : (b + 1) * SIZE, :] = kappa(v).T

        def apply(b, i, j, d):
            ahead = pick(self.cnt[i], REACH + d)
            behind = pick(self.cnt[j], REACH - d)
            vj = self.vec[j]
            vb = jnp.concatenate([vj[0:16] * ahead, vj[16:32] * behind], axis=0)
            acc[i] += jnp.dot(vb, kt[b * SIZE : (b + 1) * SIZE, :], preferred_element_type=f32)

        pairs = []
        for b in range(BAND + LAG):
            if b < BAND:
                one = b < REACH - g
                i = jnp.where(one, LEAVES + g + b, LEAVES + b - 1)
                j = jnp.where(one, LEAVES + REACH + g, EXT - 1 - g)
                pairs.append((i, j, jnp.where(one, REACH - b, 2 * REACH - b - g)))
                make(b, i, j)
            if b >= LAG:
                apply(b - LAG, *pairs[b - LAG])


NEAR_SCRATCH = [
    pltpu.VMEM((EXT, 2 * RHS, SIZE), bf16),
    pltpu.VMEM((EXT, 1, 128), f32),
    pltpu.VMEM((EXT, 2 * RHS, SIZE), f32),
    pltpu.VMEM((EXT, SIZE, 128), bf16),
    pltpu.VMEM((EXT, 16, SIZE), bf16),
    pltpu.VMEM((BAND * SIZE, SIZE), bf16),
    pltpu.VMEM((BAND * SIZE, SIZE), bf16),
    pltpu.VMEM((BAND * SIZE, SIZE), bf16),
    pltpu.VMEM((BAND * SIZE, SIZE), bf16),
    pltpu.VMEM((2 * RHS, BAND * SIZE), bf16),
    pltpu.VMEM((2 * RHS, BAND * SIZE), bf16),
]


def near_first_kernel(
    block, payload, block_far, out, arrived, halo, vec, cnt, acc, left_t, right_t, ks0, ks1, kt0, kt1, va0, va1,
    send_sem, recv_sem, own_sem, edge_send, edge_recv
):
    me = device_id()
    greet(me)
    near = Near(vec, cnt, acc, left_t, right_t, (ks0, ks1), (kt0, kt1), (va0, va1))
    acc[...] = jnp.zeros_like(acc)

    def first(j, _):
        near.features(j + REACH, block[j])
        return 0

    lax.fori_loop(0, REACH + FIRST_COLUMNS, first, 0, unroll=4)
    begin = 2 * REACH
    near.make_all(begin, 0)
    all_here()
    edges = []
    for side in range(2):
        peer = lax.rem(me + (1 if side == 0 else PEERS - 1), PEERS)
        rows = pl.ds(LEAVES - REACH, REACH) if side == 0 else pl.ds(0, REACH)
        edges.append(
            pltpu.make_async_remote_copy(
                src_ref=block_far.at[rows],
                dst_ref=halo.at[pl.ds(side * REACH, REACH)],
                send_sem=edge_send.at[side],
                recv_sem=edge_recv.at[side],
                device_id=(peer // 4, lax.rem(peer, 4)),
                device_id_type=MESH,
            )
        )
        edges[-1].start()
    send_all(me, payload, arrived, send_sem, recv_sem, own_sem)

    def body(g, _):
        j = begin + 2 * g
        near.step(j, 0, j + 1)
        near.step(j + 1, 1, j + 2)
        return 0

    lax.fori_loop(0, FIRST_COLUMNS // 2 - 1, body, 0)
    j = begin + FIRST_COLUMNS - 2
    near.step(j, 0, j + 1)
    near.step(j + 1, 1)
    out[...] = acc[REACH : REACH + LEAVES]
    for edge in edges:
        edge.wait()
    wait_all(me, payload, arrived, send_sem, recv_sem, own_sem)


def near_first(block, payload):
    return pl.pallas_call(
        near_first_kernel,
        out_shape=(
            jax.ShapeDtypeStruct((LEAVES, 2 * RHS, SIZE), f32),
            jax.ShapeDtypeStruct((PEERS, RHS, 384), bf16),
            jax.ShapeDtypeStruct((2 * REACH, ROWS, SIZE), bf16),
        ),
        in_specs=[VMEM, ANY, ANY],
        out_specs=(VMEM, ANY, ANY),
        scratch_shapes=NEAR_SCRATCH
        + [pltpu.SemaphoreType.DMA] * 3
        + [pltpu.SemaphoreType.DMA((2,)), pltpu.SemaphoreType.DMA((2,))],
        compiler_params=params(collective_id=0, has_side_effects=True),
        name="near_first",
    )(block, payload, block)


def near_rest_kernel(
    block, halo, before, ret, out, came, vec, cnt, acc, left_t, right_t, ks0, ks1, kt0, kt1, va0, va1,
    send_sem, recv_sem, own_sem
):
    me = device_id()
    greet(me)
    near = Near(vec, cnt, acc, left_t, right_t, (ks0, ks1), (kt0, kt1), (va0, va1))

    def edge(j, _):
        near.features(j, halo[j])
        near.features(j + LEAVES + REACH, halo[j + REACH])
        acc[j] = jnp.zeros((2 * RHS, SIZE), f32)
        acc[j + LEAVES + REACH] = jnp.zeros((2 * RHS, SIZE), f32)
        return 0

    lax.fori_loop(0, REACH, edge, 0, unroll=2)

    def keep(j, _):
        acc[j + REACH] = before[j]
        return 0

    lax.fori_loop(0, LEAVES, keep, 0, unroll=4)

    def first(n, _):
        j = jnp.where(n < REACH, n, n - REACH + FIRST_COLUMNS)
        near.features(j + REACH, block[j])
        return 0

    lax.fori_loop(0, REACH + LEAVES - FIRST_COLUMNS, first, 0, unroll=4)
    begin = 2 * REACH + FIRST_COLUMNS
    upper = LEAVES + REACH - begin
    columns = upper + REACH

    def column(n):
        return jnp.where(n < upper, begin + n, n - upper + REACH)

    near.make_all(begin, 0)
    all_here()
    send_all(me, ret, came, send_sem, recv_sem, own_sem)

    def body(g, _):
        near.step(column(2 * g), 0, column(2 * g + 1))
        near.step(column(2 * g + 1), 1, column(2 * g + 2))
        return 0

    lax.fori_loop(0, columns // 2 - 1, body, 0)
    near.step(column(columns - 2), 0, column(columns - 1))
    near.step(column(columns - 1), 1)

    def last(g, _):
        near.upper_edge(g)
        return 0

    lax.fori_loop(0, REACH // 2, last, 0)
    out[...] = acc[REACH : REACH + LEAVES]
    wait_all(me, ret, came, send_sem, recv_sem, own_sem)


def near_rest(block, halo, before, ret):
    return pl.pallas_call(
        near_rest_kernel,
        out_shape=(
            jax.ShapeDtypeStruct((LEAVES, 2 * RHS, SIZE), f32),
            jax.ShapeDtypeStruct((PEERS, RHS, 256), bf16),
        ),
        in_specs=[VMEM, VMEM, VMEM, ANY],
        out_specs=(VMEM, ANY),
        scratch_shapes=NEAR_SCRATCH + [pltpu.SemaphoreType.DMA] * 3,
        compiler_params=params(collective_id=1, has_side_effects=True),
        name="near_rest",
    )(block, halo, before, ret)


def far_kernel(arrived, own, back, slot, far_in, ret, feat, coef, gt0, gt1, ct0, ct1, ks0, ks1, acc_l, acc_u):
    gt, ct, ks = (gt0, gt1), (ct0, ct1), (ks0, ks1)
    low = lax.broadcasted_iota(jnp.int32, (RHS, 128), 1) < RANK
    low8 = lax.broadcasted_iota(jnp.int32, (8, 128), 1) < RANK
    tail = jnp.where(lax.broadcasted_iota(jnp.int32, (8, 128), 0) == 0, 1.0, 0.0).astype(f32)

    def both(x, mask):
        y = pltpu.roll(x, RANK, 1)
        return jnp.where(mask, x, y), jnp.where(mask, y, x)

    def table(d, _):
        for h in range(2):
            c = both(arrived[d, :, h * 128 : (h + 1) * 128].astype(f32), low)
            f = both(arrived[d, :, 256:384].astype(f32)[h * 8 : (h + 1) * 8], low8)
            for q in range(2):
                coef[d * CAP + 2 * h + q] = c[q].astype(bf16)
                feat[d * CAP + 2 * h + q] = jnp.concatenate([f[q], tail], axis=0).astype(bf16)
        return 0

    lax.fori_loop(0, PEERS, table, 0, unroll=4)
    acc_l[...] = jnp.zeros_like(acc_l)
    acc_u[...] = jnp.zeros_like(acc_u)

    def gather(i, p, t):
        for m in range(2 * t, 2 * t + 2):
            lanes = slice(m * 128, (m + 1) * 128)
            a, b = slot[i, 2 * m], slot[i, 2 * m + 1]
            gt[p][:, lanes] = jnp.where(low, feat[a], feat[b])
            ct[p][:, lanes] = jnp.where(low, coef[a], coef[b])

    def make(i, p, t):
        lanes = slice(t * 256, (t + 1) * 256)
        ks[p][:, lanes] = kappa(jnp.dot(own[i, :, 0:16], gt[p][:, lanes], preferred_element_type=f32))

    def apply(i, p, t, w):
        lanes = slice(t * 256, (t + w) * 256)
        part = lax.dot_general(ct[p][:, lanes], ks[p][:, lanes], NT, preferred_element_type=f32)
        rt = jnp.dot(back[i], ks[p][:, lanes], preferred_element_type=f32)
        for m in range(2 * w):
            tile = rt[:, m * 128 : (m + 1) * 128]
            acc_l[slot[i, 4 * t + 2 * m]] += tile
            acc_u[slot[i, 4 * t + 2 * m + 1]] += tile
        return part

    TILES = 16
    W = 2

    def step(i_next, p_next, i, p):
        total = None
        for t in range(0, TILES, W):
            part = apply(i, p, t, W)
            total = part if total is None else total + part
            for u in range(t, t + W):
                gather(i_next, p_next, u)
                make(i_next, p_next, u)
        far_in[i] = total.astype(bf16)

    for t in range(TILES):
        gather(0, 0, t)
        make(0, 0, t)

    def pair(g, _):
        step(2 * g + 1, 1, 2 * g, 0)
        step(jnp.minimum(2 * g + 2, LEAVES - 1), 0, 2 * g + 1, 1)
        return 0

    lax.fori_loop(0, LEAVES // 2, pair, 0)

    def pack(d, _):
        for h in range(2):
            s = d * CAP + 2 * h
            here = jnp.where(low, acc_l[s], acc_u[s + 1])
            over = jnp.where(low, acc_l[s + 1], acc_u[s])
            ret[d, :, h * 128 : (h + 1) * 128] = (here + pltpu.roll(over, RANK, 1)).astype(bf16)
        return 0

    lax.fori_loop(0, PEERS, pack, 0, unroll=8)


def far(arrived, own, back, slot):
    return pl.pallas_call(
        far_kernel,
        out_shape=(
            jax.ShapeDtypeStruct((LEAVES, RHS, RANK), bf16),
            jax.ShapeDtypeStruct((PEERS, RHS, 256), bf16),
        ),
        in_specs=[VMEM] * 3 + [SMEM],
        out_specs=(VMEM,) * 2,
        scratch_shapes=[
            pltpu.VMEM((SLOTS, 16, 128), bf16),
            pltpu.VMEM((SLOTS, RHS, 128), bf16),
            pltpu.VMEM((16, FAR * RANK), bf16),
            pltpu.VMEM((16, FAR * RANK), bf16),
            pltpu.VMEM((RHS, FAR * RANK), bf16),
            pltpu.VMEM((RHS, FAR * RANK), bf16),
            pltpu.VMEM((RANK, FAR * RANK), bf16),
            pltpu.VMEM((RANK, FAR * RANK), bf16),
            pltpu.VMEM((SLOTS, RHS, 128), f32),
            pltpu.VMEM((SLOTS, RHS, 128), f32),
        ],
        compiler_params=params(),
        name="far",
    )(arrived, own, back, slot)


def post_kernel(came, send, near_out, far_in, row_basis, col_basis, product, adjoint, acc_l, acc_u):
    acc_l[...] = jnp.zeros_like(acc_l)
    acc_u[...] = jnp.zeros_like(acc_u)

    def peer(d, _):
        for h in range(2):
            tile = came[d, :, h * 128 : (h + 1) * 128].astype(f32)
            acc_l[send[2 * h, d]] += tile
            acc_u[send[2 * h + 1, d]] += tile
        return 0

    lax.fori_loop(0, PEERS, peer, 0, unroll=8)

    def leaf(j, _):
        total = (acc_l[j] + pltpu.roll(acc_u[j], RANK, 1))[:, :RANK].astype(bf16)
        adjoint[j] = near_out[j, RHS:, :] + jnp.dot(total, col_basis[j], preferred_element_type=f32)
        product[j] = near_out[j, :RHS, :] + jnp.dot(far_in[j], row_basis[j], preferred_element_type=f32)
        return 0

    lax.fori_loop(0, LEAVES, leaf, 0, unroll=8)


def post(came, send, near_out, far_in, row_basis, col_basis):
    return pl.pallas_call(
        post_kernel,
        out_shape=(jax.ShapeDtypeStruct((LEAVES, RHS, SIZE), f32),) * 2,
        in_specs=[VMEM, SMEM] + [VMEM] * 4,
        out_specs=(VMEM,) * 2,
        scratch_shapes=[pltpu.VMEM((LEAVES, RHS, 128), f32)] * 2,
        compiler_params=params(),
        name="post",
    )(came, send, near_out, far_in, row_basis, col_basis)


def local(probe, weights, points, skeleton, row_basis, col_basis, near_leaf, far_slot, send_leaf):
    send = send_leaf.transpose(0, 2, 1).reshape(CAP, PEERS)
    payload, back, own, block = prep(
        probe, weights, points.transpose(1, 0, 2), skeleton, row_basis, col_basis, near_leaf.T, send
    )
    near_part, arrived, halo = near_first(block, payload)
    far_in, ret = far(arrived, own, back, far_slot)
    near_out, came = near_rest(block, halo, near_part, ret)
    return post(came, send, near_out, far_in, row_basis, col_basis)


def solution(mesh):
    lead = P(("leaf", "sub"), None, None)
    flat = P(("leaf", "sub"), None)
    return jax.shard_map(
        local,
        mesh=mesh,
        in_specs=(lead, lead, lead, flat, lead, lead, flat, flat, lead),
        out_specs=(lead, lead),
        check_vma=False,
    )
```
